256 devices in a mesh: dp: 8 (over y_hi, x), graph: 32 (over y_lo, z, core).
Axes of the slice: x: 4, y: 4 (y_hi: 2, y_lo: 2; y = y_hi * 2 + y_lo), z: 8, core: 2. Of those that a mesh axis runs over, the one named last changes fastest.
Arguments:
- nodes: bfloat16 [8, 512, 768], P('dp', 'graph'), may hold values from -6 to 6
- cotangent: bfloat16 [8, 512, 768], P('dp', 'graph'), may hold values from -16 to 16
- sources: int32 [8, 32768], P('dp', 'graph'), may hold values from 0 to 511
- targets: int32 [8, 32768], P('dp', 'graph'), may hold values from 0 to 511, as said below
- edge_weight: float32 [8, 32768], P('dp', 'graph'), may hold values from 0.2 to 1
- w_first: bfloat16 [1536, 768], replicated, may hold values from -0.15625 to 0.15625
- w_second: bfloat16 [768, 768], replicated, may hold values from -0.21875 to 0.21875
- biases: float32 [2, 768], replicated, may hold values from -3 to 3
- master: float32 [1769472], P(('dp', 'graph')), may hold values from -0.2 to 0.2
- moment_first: float32 [1769472], P(('dp', 'graph')), may hold values from -0.6 to 0.6
- moment_second: float32 [1769472], P(('dp', 'graph')), may hold values from 1 to 30
- bias_first: float32 [2, 768], replicated, may hold values from -12 to 12
- bias_second: float32 [2, 768], replicated, may hold values from 1 to 30
Outputs:
- node_out: bfloat16 [8, 512, 768], P('dp', 'graph')
- node_grad: float32 [8, 512, 768], P('dp', 'graph')
- new_master: float32 [1769472], P(('dp', 'graph'))
- new_first: float32 [1769472], P(('dp', 'graph'))
- new_second: float32 [1769472], P(('dp', 'graph'))
- new_biases: float32 [2, 768], replicated
- new_bias_first: float32 [2, 768], replicated
- new_bias_second: float32 [2, 768], replicated
The draws below stay inside these ranges and needn't reach their ends.
Inputs may be any that keep to these rules, and one draw needn't show every extreme that they name: `targets`: every node is the target of exactly 64 edges of its structure.
All inputs are finite; a program needn't handle non-finite values.
Results may differ from the reference program's by a relative error of at most 0.0031.
Values may be sent and summed in bfloat16 or wider, within the bound.
A program may use at most 64 MiB of HBM per device.

```python
import math
import jax
import jax.numpy as jnp
from jax import lax

D = 768
NODE_DEV = 16
EDGE_DEV = 1024
STEP = 10
NODES = 512
EDGES = 32768
STRUCTS = 8
PARAMS = 1769472
N_DP = 8


def shuffle_row(row_key, owner_list):
    return jax.random.permutation(row_key, owner_list)


def draw_targets(key, part):
    degree = EDGES // NODES
    owner_list = jnp.arange(EDGES, dtype=jnp.int32) // degree
    row_keys = jax.random.split(jax.random.fold_in(key, 71), STRUCTS)
    shuffled = jax.vmap(shuffle_row, in_axes=(0, None))(row_keys, owner_list)
    return shuffled.astype(jnp.int32)


def draw_cotangent(key, part):
    inner = jax.random.fold_in(key, 113)
    flat_row = jnp.arange(STRUCTS * NODES, dtype=jnp.float32).reshape(STRUCTS, NODES, 1)
    rising = 10.0 ** (flat_row / (STRUCTS * NODES - 1.0)) / 4.0
    values = jnp.clip(jax.random.normal(inner, (STRUCTS, NODES, D), jnp.float32), -6.0, 6.0)
    return (values * rising).astype(jnp.bfloat16)


def with_ends(result, key, smallest, largest):
    index_at = [jax.random.randint(jax.random.fold_in(key, axis), (), 0, length) for axis, length in enumerate(result.shape)]
    main_axis = result.shape.index(max(result.shape))
    next_to = index_at[:main_axis] + [(index_at[main_axis] + 1) % result.shape[main_axis]] + index_at[main_axis + 1:]
    return result.at[tuple(index_at)].set(smallest).at[tuple(next_to)].set(largest)


def block_scale(stream_key, extent, shards, smallest, top_value):
    def one(dim, shards_of):
        heights = jax.random.uniform(jax.random.fold_in(jax.random.fold_in(stream_key, 6), dim), (shards_of,), jnp.float32, smallest / len(shards), top_value / len(shards))
        return jnp.repeat(jnp.exp(heights), extent[dim] // shards_of).reshape((-1,) + (1,) * (len(extent) - dim - 1))

    level = one(*shards[0])
    for cut in shards[1:]:
        level = level * one(*cut)
    return level


def scatter_about(stream_key, shape, spread, limit, shards=(), kind=jnp.bfloat16):
    values = spread * jax.random.normal(stream_key, shape, jnp.float32)
    if shards:
        values = values * block_scale(stream_key, shape, shards, -0.22, 0.18)
    return jnp.clip(values, -limit, limit).astype(kind)


def setup_inputs(seed: int = 0) -> dict:
    keys = jax.random.split(jax.random.key(seed), 14)
    return {
        "nodes": scatter_about(keys[0], (STRUCTS, NODES, D), 1.0, 6.0, ((0, 8), (1, 32))),
        "cotangent": draw_cotangent(jax.random.fold_in(keys[13], 71), 0),
        "sources": with_ends(jax.random.randint(keys[2], (STRUCTS, EDGES), 0, NODES), jax.random.fold_in(keys[2], 1), 0, NODES - 1).astype(jnp.int32),
        "targets": draw_targets(jax.random.fold_in(keys[13], 71), 0),
        "edge_weight": jnp.clip(jnp.exp(math.log(1.0) - 1.609438 * jax.random.uniform(keys[4], (STRUCTS, EDGES), jnp.float32) ** block_scale(keys[4], (STRUCTS, EDGES), ((0, 8), (1, 32)), -0.2, 0.2)), 0.2, 1.0),
        "w_first": scatter_about(keys[5], (2 * D, D), (2 * D) ** -0.5, 0.15625),
        "w_second": scatter_about(keys[6], (D, D), D ** -0.5, 0.21875),
        "biases": scatter_about(keys[7], (2, D), 0.5, 3.0, (), jnp.float32),
        "master": scatter_about(keys[8], (PARAMS,), 0.03, 0.2, ((0, 256),), jnp.float32),
        "moment_first": scatter_about(keys[9], (PARAMS,), 0.1, 0.6, ((0, 256),), jnp.float32),
        "moment_second": jnp.clip(jnp.exp(math.log(30.0) - 3.4011974 * jax.random.uniform(keys[10], (PARAMS,), jnp.float32) ** block_scale(keys[10], (PARAMS,), ((0, 256),), -0.2, 0.2)), 1.0, 30.0),
        "bias_first": scatter_about(keys[11], (2, D), 2.0, 12.0, (), jnp.float32),
        "bias_second": jnp.clip(jnp.exp(jax.random.uniform(keys[12], (2, D), jnp.float32, math.log(1.0), math.log(30.0))), 1.0, 30.0),
    }


beta_one = 0.9
beta_two = 0.999
epsilon = 1e-08
learn_rate = 0.001

def structure(nodes, cotangent, sources, targets, edge_weight, w_first, w_second, biases):
    norm_scale = 1.0 / math.sqrt(EDGE_DEV / NODE_DEV)
    envelope = edge_weight[:, None]
    from_rows = nodes[sources]
    to_rows = nodes[targets]
    preact = jnp.dot(from_rows, w_first[:D], preferred_element_type=jnp.float32) + jnp.dot(to_rows, w_first[D:], preferred_element_type=jnp.float32) + biases[0]
    activation = jax.nn.silu(preact).astype(jnp.bfloat16)
    message = ((jnp.dot(activation, w_second, preferred_element_type=jnp.float32) + biases[1]) * envelope).astype(jnp.bfloat16)
    summed = jax.ops.segment_sum(message.astype(jnp.float32), targets, num_segments=NODES)
    node_out = (nodes.astype(jnp.float32) + norm_scale * summed).astype(jnp.bfloat16)
    d_out = (cotangent[targets].astype(jnp.float32) * norm_scale * envelope).astype(jnp.bfloat16)
    grad_second = jnp.dot(activation.T, d_out, preferred_element_type=jnp.float32)
    d_act = jnp.dot(d_out, w_second.T, preferred_element_type=jnp.float32)
    sigmoid_pre = jax.nn.sigmoid(preact)
    d_pre = (d_act * sigmoid_pre * (1.0 + preact * (1.0 - sigmoid_pre))).astype(jnp.bfloat16)
    grad_first = jnp.concatenate([jnp.dot(from_rows.T, d_pre, preferred_element_type=jnp.float32), jnp.dot(to_rows.T, d_pre, preferred_element_type=jnp.float32)], 0)
    d_src = jnp.dot(d_pre, w_first[:D].T, preferred_element_type=jnp.float32).astype(jnp.bfloat16)
    d_dst = jnp.dot(d_pre, w_first[D:].T, preferred_element_type=jnp.float32).astype(jnp.bfloat16)
    node_part = jax.ops.segment_sum(d_src.astype(jnp.float32), sources, num_segments=NODES) + jax.ops.segment_sum(d_dst.astype(jnp.float32), targets, num_segments=NODES)
    node_grad = cotangent.astype(jnp.float32) + node_part
    flat_grads = jnp.concatenate([grad_first.reshape(-1), grad_second.reshape(-1)])
    bias_terms = jnp.stack([lax.optimization_barrier(jnp.sum(d_pre.astype(jnp.float32), 0)), lax.optimization_barrier(jnp.sum(d_out.astype(jnp.float32), 0))])
    return (node_out, node_grad, flat_grads, bias_terms)

def adam_update(param, first, second, grads):
    new_first = beta_one * first + (1.0 - beta_one) * grads
    new_second = beta_two * second + (1.0 - beta_two) * grads * grads
    ratio = new_first / (1.0 - beta_one ** STEP) / (jnp.sqrt(new_second / (1.0 - beta_two ** STEP)) + epsilon)
    return (param - learn_rate * ratio, new_first, new_second)

def reference(nodes, cotangent, sources, targets, edge_weight, w_first, w_second, biases, master, moment_first, moment_second, bias_first, bias_second):

    def one_struct(inputs):
        return structure(inputs[0], inputs[1], inputs[2], inputs[3], inputs[4], w_first, w_second, biases)
    node_out, node_grad, flat_grads, bias_terms = lax.map(one_struct, (nodes, cotangent, sources, targets, edge_weight))
    grads = lax.optimization_barrier(jnp.sum(flat_grads, 0)) / N_DP
    bias_grads = lax.optimization_barrier(jnp.sum(bias_terms, 0)) / N_DP
    new_master, new_first, new_second = adam_update(master, moment_first, moment_second, grads)
    new_biases, new_bias_first, new_bias_second = adam_update(biases, bias_first, bias_second, bias_grads)
    return (node_out, node_grad, new_master, new_first, new_second, new_biases, new_bias_first, new_bias_second)
```

```python
import math

import jax
import jax.numpy as jnp
from jax import lax
from jax.experimental import pallas as pl
from jax.experimental.pallas import tpu as pltpu
from jax.sharding import PartitionSpec as P

STEP = 10


beta_one = 0.9
beta_two = 0.999
epsilon = 1e-08
learn_rate = 0.001

D = 768
ROWS = 16
EDGE = 1024
NZ = 8
C = D // NZ
NODES = 512
BF = jnp.bfloat16
F32 = jnp.float32
NN = (((1,), (0,)), ((), ()))
NT = (((1,), (1,)), ((), ()))
TN = (((0,), (0,)), ((), ()))


def mm(a, b, dims=NN):
    return lax.dot_general(a, b, dims, preferred_element_type=F32)


def split(x):
    hi = x.astype(BF)
    return hi, (x - hi.astype(F32)).astype(BF)


def adam_update(param, first, second, grads):
    new_first = beta_one * first + (1.0 - beta_one) * grads
    new_second = beta_two * second + (1.0 - beta_two) * grads * grads
    ratio = (
        new_first
        / (1.0 - beta_one**STEP)
        / (jnp.sqrt(new_second / (1.0 - beta_two**STEP)) + epsilon)
    )
    return (param - learn_rate * ratio, new_first, new_second)


def layer_kernel(
    norm_scale,
    nodes_hbm,
    cot_hbm,
    src_hbm,
    tgt_hbm,
    weight_hbm,
    w1_hbm,
    w2_hbm,
    bias_hbm,
    out_ref,
    grad_ref,
    gsum_ref,
    nodes_ref,
    cot_ref,
    src_ref,
    tgt_ref,
    weight_ref,
    w1_ref,
    w2_ref,
    bias_ref,
    feats,
    edges,
    psrc,
    ptgt,
    onehot_s,
    onehot_t,
    row,
    part,
    part_in,
    half_out,
    half_in,
    total,
    own,
    cols,
    sw_out,
    sw_in,
    gout,
    gin,
    y_send,
    y_recv,
    z_send,
    z_recv,
    c_send,
    c_recv,
    r_send,
    r_recv,
    a_send,
    a_recv,
    z2_send,
    z2_recv,
    c2_send,
    c2_recv,
    d_send,
    d_recv,
    l_sem,
):
    dp = lax.axis_index("dp")
    graph = lax.axis_index("graph")
    y = graph // 16
    z = (graph // 2) % 8
    c = graph % 2

    def peer(py, pz, pc):
        return {"dp": dp, "graph": py * 16 + pz * 2 + pc}

    def zat(k):
        return (z + k + 8) % 8

    y_peer = peer(1 - y, z, c)
    c_peer = peer(y, z, 1 - c)
    right = peer(y, zat(1), c)
    left = peer(y, zat(-1), c)

    loads = [
        pltpu.make_async_copy(src, dst, l_sem.at[i])
        for i, (src, dst) in enumerate(
            [
                (nodes_hbm, nodes_ref),
                (cot_hbm, cot_ref),
                (src_hbm, src_ref),
                (tgt_hbm, tgt_ref),
                (weight_hbm, weight_ref),
                (bias_hbm, bias_ref),
                (w1_hbm, w1_ref),
                (w2_hbm, w2_ref),
            ]
        )
    ]
    for load in loads:
        load.start()

    barrier = pltpu.get_barrier_semaphore()
    greet = [y_peer, c_peer] + [peer(y, zat(k), c) for k in range(1, 8)]
    greet += [{"dp": (dp + k) % 8, "graph": graph} for k in range(1, 8)]
    for who in greet:
        pl.semaphore_signal(barrier, inc=1, device_id=who, device_id_type=pl.DeviceIdType.MESH)

    def remote(src, dst, send, recv, who):
        return pltpu.make_async_remote_copy(
            src_ref=src,
            dst_ref=dst,
            send_sem=send,
            recv_sem=recv,
            device_id=who,
            device_id_type=pl.DeviceIdType.MESH,
        )

    pending = []

    def send(src, dst, ssem, rsem, who):
        copy = remote(src, dst, ssem, rsem, who)
        copy.start()
        pending.append(copy)

    def arrived(dst, ssem, rsem):
        remote(dst, dst, ssem, rsem, right).wait_recv()

    for load in loads[0:5]:
        load.wait()
    zrow = pl.multiple_of(z * ROWS, ROWS)
    feats[0, c, y, pl.ds(zrow, ROWS), :] = nodes_ref[0]
    feats[1, c, y, pl.ds(zrow, ROWS), :] = cot_ref[0]

    def place(n):
        ny, nz, nc, nr = n // 256, (n // 32) % 8, (n // 16) % 2, n % 16
        return nc * 256 + ny * 128 + nz * 16 + nr

    for j in range(8):
        lanes = slice(j * 128, (j + 1) * 128)
        edges[z, j : j + 1, :] = place(src_ref[0:1, lanes]).astype(F32)
        edges[z, 8 + j : 9 + j, :] = place(tgt_ref[0:1, lanes]).astype(F32)
        edges[z, 16 + j : 17 + j, :] = weight_ref[0:1, lanes]

    pl.semaphore_wait(barrier, len(greet))

    def slot(kind, at):
        if kind == 2:
            return edges.at[at]
        return feats.at[kind, c, :, pl.ds(pl.multiple_of(at * ROWS, ROWS), ROWS), :]

    def other_slot(kind, at):
        return feats.at[kind, 1 - c, :, pl.ds(pl.multiple_of(at * ROWS, ROWS), ROWS), :]

    for kind in range(2):
        mine = feats.at[kind, c, y, pl.ds(zrow, ROWS), :]
        send(mine, mine, y_send.at[kind], y_recv.at[kind], y_peer)

    def to_right(kind, k):
        ref = slot(kind, zat(-k))
        send(ref, ref, z_send.at[0, k, kind], z_recv.at[0, k, kind], right)

    def to_left(kind, k):
        ref = slot(kind, zat(k))
        send(ref, ref, z_send.at[1, k, kind], z_recv.at[1, k, kind], left)

    def to_core(kind, k):
        ref = slot(kind, zat(k))
        send(ref, ref, c_send.at[k % 8, kind], c_recv.at[k % 8, kind], c_peer)

    to_right(2, 0)
    to_left(2, 0)

    for load in loads[5:8]:
        load.wait()
    pick = lax.broadcasted_iota(jnp.int32, (C, D), 1) == (
        lax.broadcasted_iota(jnp.int32, (C, D), 0) + z * C
    )
    pick_bf = jnp.where(pick, 1.0, 0.0).astype(BF)
    w1s_cols = mm(pick_bf, w1_ref[0:D, :], NT).astype(BF)
    w1t_cols = mm(pick_bf, w1_ref[D : 2 * D, :], NT).astype(BF)
    b0 = jnp.sum(jnp.where(pick, bias_ref[0:1, :], 0.0), axis=1, keepdims=True)

    for kind in range(2):
        theirs = feats.at[kind, c, 1 - y, pl.ds(zrow, ROWS), :]
        arrived(theirs, y_send.at[kind], y_recv.at[kind])
        to_right(kind, 0)
        to_left(kind, 0)
        to_core(kind, 0)
    for k in range(1, 5):
        for kind in (2, 0, 1):
            arrived(slot(kind, zat(-k)), z_send.at[0, k - 1, kind], z_recv.at[0, k - 1, kind])
            if k < 4:
                to_right(kind, k)
            if kind < 2:
                to_core(kind, -k)
            if k < 4:
                arrived(slot(kind, zat(k)), z_send.at[1, k - 1, kind], z_recv.at[1, k - 1, kind])
                if k < 3:
                    to_left(kind, k)
                if kind < 2:
                    to_core(kind, k)
    for kind in range(2):
        for k in range(8):
            arrived(other_slot(kind, zat(k)), c_send.at[k, kind], c_recv.at[k, kind])

    all_nodes = feats[0].reshape(NODES, D)
    all_cot = feats[1].reshape(NODES, D)
    hi, lo = split(mm(w1s_cols, all_nodes, NT))
    psrc[0:C] = hi
    psrc[C : 2 * C] = lo
    hi, lo = split(mm(w1t_cols, all_nodes, NT))
    ptgt[0:C] = hi
    ptgt[C : 2 * C] = lo
    w2_cols = w2_ref[pl.ds(pl.multiple_of(z * C, 16), C), :]
    ptgt[2 * C : 3 * C] = (norm_scale * mm(w2_cols, all_cot, NT)).astype(BF)

    part[...] = jnp.zeros_like(part)

    def edge_block(i, carry):
        ids = lax.broadcasted_iota(jnp.int32, (NODES, 128), 0).astype(F32)
        for j in range(8):
            lanes = slice(j * 128, (j + 1) * 128)
            onehot_s[:, lanes] = jnp.where(ids == edges[i, j : j + 1, :], 1.0, 0.0).astype(BF)
            onehot_t[:, lanes] = jnp.where(ids == edges[i, 8 + j : 9 + j, :], 1.0, 0.0).astype(BF)
            row[0:1, lanes] = edges[i, 16 + j : 17 + j, :]
        w = row[0:1, :]
        u = mm(psrc[...], onehot_s[...])
        v = mm(ptgt[...], onehot_t[...])
        pre = (u[0:C] + v[0:C]) + (u[C : 2 * C] + v[C : 2 * C]) + b0
        sg = 0.5 * jnp.tanh(0.5 * pre) + 0.5
        act = pre * sg
        dpre = ((v[2 * C : 3 * C] * w) * (sg * (1.0 + pre - act))).astype(BF)
        w_hi, w_lo = split(w)
        rank = lax.broadcasted_iota(jnp.int32, (128 - C, EDGE), 0)
        tail = jnp.where(rank == 0, w_hi.astype(F32), jnp.where(rank == 1, w_lo.astype(F32), 0.0))
        zeros = jnp.zeros((128 - C, EDGE), BF)
        to_t = jnp.concatenate([(act * w).astype(BF), tail.astype(BF), dpre, zeros], 0)
        to_s = jnp.concatenate([dpre, zeros], 0)
        at = mm(onehot_t[...], to_t, NT)
        s = mm(onehot_s[...], to_s, NT)
        for h in range(2):
            rows = slice(h * 256, (h + 1) * 256)
            part[h, :, 0:128] += at[rows, 0:128]
            part[h, :, 256:384] += at[rows, 128:256]
            part[h, :, 128:256] += s[rows, :]
        return carry

    lax.fori_loop(0, NZ, edge_block, 0)

    send(part.at[1 - c], part_in, r_send.at[0], r_recv.at[0], c_peer)
    arrived(part_in, r_send.at[0], r_recv.at[0])
    half_out[...] = (part[c] + part_in[...]).astype(BF)
    send(half_out, half_in, r_send.at[1], r_recv.at[1], y_peer)

    at_row = lax.broadcasted_iota(jnp.int32, (128, D), 0)
    at_col = lax.broadcasted_iota(jnp.int32, (128, D), 1)
    wanted = jnp.where(at_row % 16 < 9, (at_row // 16) * 288 + graph * 9 + at_row % 16, -1)

    def chosen(block):
        return jnp.where(wanted == at_col + block * D, 1.0, 0.0).astype(BF)

    in_block = lax.broadcasted_iota(jnp.int32, (128, NODES), 0) % 16
    x_src = mm(chosen(0), all_nodes, NT).astype(BF)
    x_tgt = jnp.where(in_block == 9, 1.0, mm(chosen(1), all_nodes, NT)).astype(BF)

    arrived(half_in, r_send.at[1], r_recv.at[1])
    total[...] = half_out[...].astype(F32) + half_in[...].astype(F32)

    own[z] = total[pl.ds(pl.multiple_of(y * 128 + z * ROWS, ROWS), ROWS), :]
    for k in range(1, 8):
        rows = pl.ds(pl.multiple_of(y * 128 + zat(k) * ROWS, ROWS), ROWS)
        send(total.at[rows, :], own.at[z], a_send.at[k], a_recv.at[k], peer(y, zat(k), c))

    def block(at, pc):
        rows = pl.ds(pl.multiple_of(at * C, 16), C)
        return cols.at[:, rows, pl.ds(pl.multiple_of(pc * 256, 256), 256)]

    zc = pl.ds(pl.multiple_of(z * C, 16), C)
    for kind in range(3):
        flipped = total[:, kind * 128 : (kind + 1) * 128].T
        cols[kind, zc, pl.ds(pl.multiple_of(c * 256, 256), 256)] = flipped[0:C].astype(BF)
        if kind == 0:
            sw_out[...] = flipped[C : C + 8]
            send(sw_out, sw_in, r_send.at[2], r_recv.at[2], c_peer)

    def to_right2(k):
        ref = block(zat(-k), c)
        send(ref, ref, z2_send.at[0, k], z2_recv.at[0, k], right)

    def to_left2(k):
        ref = block(zat(k), c)
        send(ref, ref, z2_send.at[1, k], z2_recv.at[1, k], left)

    def to_core2(k):
        ref = block(zat(k), c)
        send(ref, ref, c2_send.at[k % 8], c2_recv.at[k % 8], c_peer)

    to_right2(0)
    to_left2(0)
    to_core2(0)

    for k in range(1, 5):
        arrived(block(zat(-k), c), z2_send.at[0, k - 1], z2_recv.at[0, k - 1])
        if k < 4:
            to_right2(k)
        to_core2(-k)
        if k < 4:
            arrived(block(zat(k), c), z2_send.at[1, k - 1], z2_recv.at[1, k - 1])
            if k < 3:
                to_left2(k)
            to_core2(k)
    for k in range(8):
        arrived(block(zat(k), 1 - c), c2_send.at[k], c2_recv.at[k])

    for k in range(1, 8):
        arrived(own.at[zat(-k)], a_send.at[k], a_recv.at[k])
    arrived(sw_in, r_send.at[2], r_recv.at[2])
    sw_mine = sw_out[0:1] + sw_out[1:2]
    sw_theirs = sw_in[0:1] + sw_in[1:2]
    first = jnp.where(c == 0, sw_mine, sw_theirs)
    second = jnp.where(c == 0, sw_theirs, sw_mine)
    sw_hi, sw_lo = split(jnp.concatenate([first, second], 1))

    x_act = mm(chosen(2), cols[0])
    x_act = jnp.where(in_block == 10, sw_hi.astype(F32), x_act)
    x_act = jnp.where(in_block == 11, sw_lo.astype(F32), x_act).astype(BF)
    grads = mm(x_src, cols[1], NT) + mm(x_tgt, cols[2], NT) + norm_scale * mm(x_act, all_cot)
    gout[...] = grads.reshape(8, 16, D)
    gin[dp] = gout[dp]
    for k in range(1, 8):
        to = (dp + k) % 8
        send(gout.at[to], gin.at[dp], d_send.at[k], d_recv.at[k], {"dp": to, "graph": graph})

    summed = jnp.zeros((ROWS, D), F32)
    back = jnp.zeros((ROWS, D), F32)
    for k in range(8):
        piece = own[k]
        rows = slice(k * C, (k + 1) * C)
        a = jnp.concatenate(split(piece[:, 0:C]), 0)
        m = mm(a, w2_ref[rows, :])
        summed += m[0:ROWS] + m[ROWS : 2 * ROWS]
        for kind in (1, 2):
            g = jnp.concatenate(split(piece[:, kind * 128 : kind * 128 + C]), 0)
            m = mm(g, w1_ref[(kind - 1) * D : kind * D, rows], NT)
            back += m[0:ROWS] + m[ROWS : 2 * ROWS]
    sw = own[0, :, C : C + 1] + own[0, :, C + 1 : C + 2]
    summed += sw * bias_ref[1:2, :]
    out_ref[0] = (nodes_ref[0].astype(F32) + norm_scale * summed).astype(BF)
    grad_ref[0] = cot_ref[0].astype(F32) + back

    for k in range(1, 8):
        arrived(gin.at[(dp - k + 8) % 8], d_send.at[k], d_recv.at[k])
    acc = gin[0]
    for k in range(1, 8):
        acc += gin[k]
    gsum_ref[...] = acc

    for copy in pending:
        copy.wait_send()


def shards(
    nodes,
    cotangent,
    sources,
    targets,
    edge_weight,
    w_first,
    w_second,
    biases,
    master,
    moment_first,
    moment_second,
    bias_first,
    bias_second,
):
    norm_scale = 1.0 / math.sqrt(sources.shape[1] / nodes.shape[1])
    groups = lax.axis_size("dp")

    def kernel(*refs):
        layer_kernel(norm_scale, *refs)

    vmem = pl.BlockSpec(memory_space=pltpu.VMEM)
    dma = pltpu.SemaphoreType.DMA
    node_out, node_grad, gsum = pl.pallas_call(
        kernel,
        out_shape=(
            jax.ShapeDtypeStruct((1, ROWS, D), BF),
            jax.ShapeDtypeStruct((1, ROWS, D), F32),
            jax.ShapeDtypeStruct((ROWS, D), F32),
        ),
        in_specs=[pl.BlockSpec(memory_space=pltpu.HBM)] * 8,
        out_specs=(vmem, vmem, vmem),
        scratch_shapes=[
            pltpu.VMEM((1, ROWS, D), BF),
            pltpu.VMEM((1, ROWS, D), BF),
            pltpu.VMEM((1, EDGE), jnp.int32),
            pltpu.VMEM((1, EDGE), jnp.int32),
            pltpu.VMEM((1, EDGE), F32),
            pltpu.VMEM((2 * D, D), BF),
            pltpu.VMEM((D, D), BF),
            pltpu.VMEM((2, D), F32),
            pltpu.VMEM((2, 2, 2, 128, D), BF),
            pltpu.VMEM((NZ, 24, 128), F32),
            pltpu.VMEM((2 * C, NODES), BF),
            pltpu.VMEM((3 * C, NODES), BF),
            pltpu.VMEM((NODES, EDGE), BF),
            pltpu.VMEM((NODES, EDGE), BF),
            pltpu.VMEM((8, EDGE), F32),
            pltpu.VMEM((2, 256, 384), F32),
            pltpu.VMEM((256, 384), F32),
            pltpu.VMEM((256, 384), BF),
            pltpu.VMEM((256, 384), BF),
            pltpu.VMEM((256, 384), F32),
            pltpu.VMEM((NZ, ROWS, 384), F32),
            pltpu.VMEM((3, D, NODES), BF),
            pltpu.VMEM((8, 256), F32),
            pltpu.VMEM((8, 256), F32),
            pltpu.VMEM((8, ROWS, D), F32),
            pltpu.VMEM((8, ROWS, D), F32),
            dma((2,)),
            dma((2,)),
            dma((2, 4, 3)),
            dma((2, 4, 3)),
            dma((8, 2)),
            dma((8, 2)),
            dma((3,)),
            dma((3,)),
            dma((8,)),
            dma((8,)),
            dma((2, 4)),
            dma((2, 4)),
            dma((8,)),
            dma((8,)),
            dma((8,)),
            dma((8,)),
            dma((8,)),
        ],
        compiler_params=pltpu.CompilerParams(
            collective_id=0, has_side_effects=True, vmem_limit_bytes=63 * 1024 * 1024
        ),
        name="layer",
    )(nodes, cotangent, sources, targets, edge_weight, w_first, w_second, biases)

    grads = gsum[0:9].reshape(-1) / groups
    bias_grads = jnp.stack([gsum[9], gsum[10] + gsum[11]]) / groups
    new_master, new_first, new_second = adam_update(master, moment_first, moment_second, grads)
    new_biases, new_bias_first, new_bias_second = adam_update(
        biases, bias_first, bias_second, bias_grads
    )
    return (
        node_out,
        node_grad,
        new_master,
        new_first,
        new_second,
        new_biases,
        new_bias_first,
        new_bias_second,
    )


def solution(mesh):
    placed = (
        P("dp", "graph", None),
        P("dp", "graph", None),
        P("dp", "graph"),
        P("dp", "graph"),
        P("dp", "graph"),
        P(),
        P(),
        P(),
        P(("dp", "graph")),
        P(("dp", "graph")),
        P(("dp", "graph")),
        P(),
        P(),
    )
    return jax.shard_map(
        shards,
        mesh=mesh,
        in_specs=placed,
        out_specs=(
            P("dp", "graph", None),
            P("dp", "graph", None),
            P(("dp", "graph")),
            P(("dp", "graph")),
            P(("dp", "graph")),
            P(),
            P(),
            P(),
        ),
        check_vma=False,
    )
```

```python
import math

import jax
import jax.numpy as jnp
from jax import lax
from jax.experimental import pallas as pl
from jax.experimental.pallas import tpu as pltpu
from jax.sharding import PartitionSpec as P

STEP = 10


beta_one = 0.9
beta_two = 0.999
epsilon = 1e-08
learn_rate = 0.001

D = 768
ROWS = 16
EDGE = 1024
NZ = 8
W = 112
NODES = 512
BF = jnp.bfloat16
F32 = jnp.float32
NN = (((1,), (0,)), ((), ()))
NT = (((1,), (1,)), ((), ()))
TN = (((0,), (0,)), ((), ()))


def mm(a, b, dims=NN):
    return lax.dot_general(a, b, dims, preferred_element_type=F32)


def split(x):
    hi = x.astype(BF)
    return hi, (x - hi.astype(F32)).astype(BF)


def adam_update(param, first, second, grads):
    new_first = beta_one * first + (1.0 - beta_one) * grads
    new_second = beta_two * second + (1.0 - beta_two) * grads * grads
    ratio = (
        new_first
        / (1.0 - beta_one**STEP)
        / (jnp.sqrt(new_second / (1.0 - beta_two**STEP)) + epsilon)
    )
    return (param - learn_rate * ratio, new_first, new_second)


def column_of(z, i):
    owner = ((i % 36) // 18) * 16 + z * 2 + ((i % 18) // 9)
    h = (5 + i // 36) * 288 + owner * 9 + i % 9 - 2 * D
    return jnp.where((i < 108) & (h >= 0), h, -1)


def layer_kernel(
    norm_scale,
    nodes_hbm,
    cot_hbm,
    src_hbm,
    tgt_hbm,
    weight_hbm,
    w1_hbm,
    w2_hbm,
    bias_hbm,
    out_ref,
    grad_ref,
    gsum_ref,
    nodes_ref,
    cot_ref,
    src_ref,
    tgt_ref,
    weight_ref,
    w1_ref,
    w2_ref,
    bias_ref,
    feats,
    edges,
    perm,
    prod_out,
    prod,
    psrc,
    ptgt,
    onehot_s,
    onehot_t,
    row,
    part,
    part_in,
    half_out,
    half_in,
    total,
    own,
    flip,
    g1,
    g1_in,
    g1_sum,
    g1_out,
    g1_last,
    g2,
    g2_in,
    bias_out,
    bias_in,
    bias_mine,
    bias_last,
    y_send,
    y_recv,
    z_send,
    z_recv,
    c_send,
    c_recv,
    e_send,
    e_recv,
    p_send,
    p_recv,
    r_send,
    r_recv,
    a_send,
    a_recv,
    d_send,
    d_recv,
    f_send,
    f_recv,
    b_send,
    b_recv,
    l_sem,
):
    dp = lax.axis_index("dp")
    graph = lax.axis_index("graph")
    y = graph // 16
    z = (graph // 2) % 8
    c = graph % 2
    quarter = y * 2 + c

    def peer(py, pz, pc):
        return {"dp": dp, "graph": py * 16 + pz * 2 + pc}

    def zat(k):
        return (z + k + 8) % 8

    y_peer = peer(1 - y, z, c)
    c_peer = peer(y, z, 1 - c)
    right = peer(y, zat(1), c)
    left = peer(y, zat(-1), c)

    loads = [
        pltpu.make_async_copy(src, dst, l_sem.at[i])
        for i, (src, dst) in enumerate(
            [
                (nodes_hbm, nodes_ref),
                (cot_hbm, cot_ref),
                (src_hbm, src_ref),
                (tgt_hbm, tgt_ref),
                (weight_hbm, weight_ref),
                (bias_hbm, bias_ref),
                (w1_hbm, w1_ref),
                (w2_hbm, w2_ref),
            ]
        )
    ]
    for load in loads:
        load.start()

    barrier = pltpu.get_barrier_semaphore()
    greet = [y_peer, c_peer]
    for k in range(1, 8):
        greet += [peer(y, zat(k), c), peer(y, zat(k), 1 - c), {"dp": (dp + k) % 8, "graph": graph}]
    for who in greet:
        pl.semaphore_signal(barrier, inc=1, device_id=who, device_id_type=pl.DeviceIdType.MESH)

    def remote(src, dst, send, recv, who):
        return pltpu.make_async_remote_copy(
            src_ref=src,
            dst_ref=dst,
            send_sem=send,
            recv_sem=recv,
            device_id=who,
            device_id_type=pl.DeviceIdType.MESH,
        )

    pending = []

    def send(src, dst, ssem, rsem, who, when=None):
        copy = remote(src, dst, ssem, rsem, who)
        if when is None:
            copy.start()
        else:
            pl.when(when)(copy.start)
        pending.append((copy, when))

    def arrived(dst, ssem, rsem):
        remote(dst, dst, ssem, rsem, right).wait_recv()

    at_h = lax.broadcasted_iota(jnp.int32, (D, 128), 0)
    for k in range(8):
        place_of = column_of(k, lax.broadcasted_iota(jnp.int32, (1, 128), 1))
        perm[:, k * 128 : (k + 1) * 128] = jnp.where(at_h == place_of, 1.0, 0.0).astype(BF)

    for load in loads[0:5]:
        load.wait()
    zrow = pl.multiple_of(z * ROWS, ROWS)
    feats[0, c, y, pl.ds(zrow, ROWS), :] = nodes_ref[0]
    feats[1, c, y, pl.ds(zrow, ROWS), :] = cot_ref[0]

    def place(n):
        ny, nz, nc, nr = n // 256, (n // 32) % 8, (n // 16) % 2, n % 16
        return nc * 256 + ny * 128 + nz * 16 + nr

    for j in range(8):
        lanes = slice(j * 128, (j + 1) * 128)
        edges[z, j : j + 1, :] = place(src_ref[0:1, lanes]).astype(F32)
        edges[z, 8 + j : 9 + j, :] = place(tgt_ref[0:1, lanes]).astype(F32)
        edges[z, 16 + j : 17 + j, :] = weight_ref[0:1, lanes]

    for load in loads[5:8]:
        load.wait()
    from_s = mm(nodes_ref[0], w1_ref[0:D, :]).astype(BF)
    from_t = split(mm(nodes_ref[0], w1_ref[D : 2 * D, :]))
    from_c = (norm_scale * mm(cot_ref[0], w2_ref[...], NT)).astype(BF)
    stack = jnp.concatenate([from_s, from_t[0], from_t[1], from_c], 0)
    spread = mm(stack, perm[...])
    for k in range(8):
        for kind in range(4):
            rows = slice(kind * ROWS, (kind + 1) * ROWS)
            prod_out[k, kind] = spread[rows, k * 128 : (k + 1) * 128].astype(BF)

    pl.semaphore_wait(barrier, len(greet))

    def zbase(pc, py, pz):
        return pl.multiple_of(pc * 256 + py * 128 + pz * ROWS, ROWS)

    def products(pc, py, pz):
        return prod.at[:, pl.ds(zbase(pc, py, pz), ROWS), :]

    for k in range(1, 8):
        to = peer(y, zat(k), c)
        send(prod_out.at[zat(k)], products(c, y, z), p_send.at[0, k], p_recv.at[0, k], to)
        send(edges.at[z], edges.at[z], e_send.at[k], e_recv.at[k], to)
    prod[:, pl.ds(zbase(c, y, z), ROWS), :] = prod_out[z]

    def slot(kind, at):
        return feats.at[kind, c, :, pl.ds(pl.multiple_of(at * ROWS, ROWS), ROWS), :]

    def other_slot(kind, at):
        return feats.at[kind, 1 - c, :, pl.ds(pl.multiple_of(at * ROWS, ROWS), ROWS), :]

    for k in range(8):
        ref = products(c, y, zat(-k))
        if k:
            arrived(ref, p_send.at[0, k], p_recv.at[0, k])
        send(ref, ref, p_send.at[1, k], p_recv.at[1, k], y_peer)
        send(ref, ref, p_send.at[2, k], p_recv.at[2, k], c_peer)
    for kind in range(2):
        mine = feats.at[kind, c, y, pl.ds(zrow, ROWS), :]
        send(mine, mine, y_send.at[kind], y_recv.at[kind], y_peer)
    for k in range(8):
        ref = products(c, 1 - y, zat(-k))
        arrived(ref, p_send.at[1, k], p_recv.at[1, k])
        send(ref, ref, p_send.at[3, k], p_recv.at[3, k], c_peer)

    def to_right(kind, k):
        ref = slot(kind, zat(-k))
        send(ref, ref, z_send.at[0, k, kind], z_recv.at[0, k, kind], right)

    def to_left(kind, k):
        ref = slot(kind, zat(k))
        send(ref, ref, z_send.at[1, k, kind], z_recv.at[1, k, kind], left)

    def to_core(kind, k):
        ref = slot(kind, zat(k))
        send(ref, ref, c_send.at[k % 8, kind], c_recv.at[k % 8, kind], c_peer)

    for kind in range(2):
        theirs = feats.at[kind, c, 1 - y, pl.ds(zrow, ROWS), :]
        arrived(theirs, y_send.at[kind], y_recv.at[kind])
        to_right(kind, 0)
        to_left(kind, 0)
        to_core(kind, 0)

    def ring(k):
        for kind in range(2):
            arrived(slot(kind, zat(-k)), z_send.at[0, k - 1, kind], z_recv.at[0, k - 1, kind])
            if k < 4:
                to_right(kind, k)
            to_core(kind, -k)
            if k < 4:
                arrived(slot(kind, zat(k)), z_send.at[1, k - 1, kind], z_recv.at[1, k - 1, kind])
                if k < 3:
                    to_left(kind, k)
                to_core(kind, k)

    pick = lax.broadcasted_iota(jnp.int32, (W, D), 1) == column_of(
        z, lax.broadcasted_iota(jnp.int32, (W, 1), 0)
    )
    b0 = jnp.sum(jnp.where(pick, bias_ref[0:1, :], 0.0), axis=1, keepdims=True)
    part[...] = jnp.zeros_like(part)

    for k in range(1, 8):
        arrived(edges.at[zat(-k)], e_send.at[k], e_recv.at[k])
    for k in range(8):
        arrived(products(1 - c, y, zat(-k)), p_send.at[2, k], p_recv.at[2, k])
        arrived(products(1 - c, 1 - y, zat(-k)), p_send.at[3, k], p_recv.at[3, k])

    psrc[...] = prod[0].astype(F32).T[0:W].astype(BF)
    for kind in range(3):
        ptgt[kind * W : (kind + 1) * W] = prod[kind + 1].astype(F32).T[0:W].astype(BF)

    def edge_block(i, carry):
        ids = lax.broadcasted_iota(jnp.int32, (NODES, 128), 0).astype(F32)
        for j in range(8):
            lanes = slice(j * 128, (j + 1) * 128)
            onehot_s[:, lanes] = jnp.where(ids == edges[i, j : j + 1, :], 1.0, 0.0).astype(BF)
            onehot_t[:, lanes] = jnp.where(ids == edges[i, 8 + j : 9 + j, :], 1.0, 0.0).astype(BF)
            row[0:1, lanes] = edges[i, 16 + j : 17 + j, :]
        w = row[0:1, :]
        u = mm(psrc[...], onehot_s[...])
        v = mm(ptgt[...], onehot_t[...])
        pre = (u + v[0:W]) + v[W : 2 * W] + b0
        sg = 0.5 * jnp.tanh(0.5 * pre) + 0.5
        act = pre * sg
        dpre = ((v[2 * W : 3 * W] * w) * (sg * (1.0 + pre - act))).astype(BF)
        w_hi, w_lo = split(w)
        rank = lax.broadcasted_iota(jnp.int32, (128 - W, EDGE), 0)
        tail = jnp.where(rank == 0, w_hi.astype(F32), jnp.where(rank == 1, w_lo.astype(F32), 0.0))
        zeros = jnp.zeros((128 - W, EDGE), BF)
        to_t = jnp.concatenate([(act * w).astype(BF), tail.astype(BF), dpre, zeros], 0)
        to_s = jnp.concatenate([dpre, zeros], 0)
        at = mm(onehot_t[...], to_t, NT)
        s = mm(onehot_s[...], to_s, NT)
        for h in range(2):
            rows = slice(h * 256, (h + 1) * 256)
            part[h, :, 0:128] += at[rows, 0:128]
            part[h, :, 256:384] += at[rows, 128:256]
            part[h, :, 128:256] += s[rows, :]
        return carry

    for k in range(4):
        lax.fori_loop(2 * k, 2 * k + 2, edge_block, 0)
        ring(k + 1)

    send(part.at[1 - c], part_in, r_send.at[0], r_recv.at[0], c_peer)
    arrived(part_in, r_send.at[0], r_recv.at[0])
    half_out[...] = (part[c] + part_in[...]).astype(BF)
    send(half_out, half_in, r_send.at[1], r_recv.at[1], y_peer)

    for kind in range(2):
        for k in range(8):
            arrived(other_slot(kind, zat(k)), c_send.at[k, kind], c_recv.at[k, kind])
    flip[...] = feats[0].reshape(NODES, D).astype(F32).T.astype(BF)
    lane = lax.broadcasted_iota(jnp.int32, (48, 128), 1)
    mine = lax.broadcasted_iota(jnp.int32, (48, 128), 0)
    wanted = jnp.where(mine % 16 < 9, (mine // 16) * 36 + quarter * 9 + mine % 16, -1)
    chosen = jnp.where(lane == wanted, 1.0, 0.0).astype(BF)

    arrived(half_in, r_send.at[1], r_recv.at[1])
    total[c] = half_out[...].astype(F32) + half_in[...].astype(F32)
    send(total.at[c], total.at[c], r_send.at[2], r_recv.at[2], c_peer)

    own[z] = total[c, pl.ds(pl.multiple_of(y * 128 + z * ROWS, ROWS), ROWS), :]
    for k in range(1, 8):
        rows = pl.ds(pl.multiple_of(y * 128 + zat(k) * ROWS, ROWS), ROWS)
        send(total.at[c, rows, :], own.at[z], a_send.at[k], a_recv.at[k], peer(y, zat(k), c))

    arrived(total.at[1 - c], r_send.at[2], r_recv.at[2])

    def sums(kind):
        return total[:, :, kind * 128 : (kind + 1) * 128].reshape(NODES, 128)

    sum_a, sum_s, sum_t = sums(0), sums(1), sums(2)
    for kind, x in enumerate((sum_s, sum_t)):
        m = mm(flip[...], jnp.concatenate(split(x), 1))
        g1[kind * D : (kind + 1) * D, :] = m[:, 0:128] + m[:, 128:256]
    g1[2 * D :, :] = jnp.zeros((6 * 288 - 2 * D, 128), F32)

    def others():
        return [(k, (dp + k) % 8) for k in range(1, 8)]

    def chunk(to):
        return pl.ds(pl.multiple_of(to * 288 + quarter * 72, 8), 72)

    for k, to in others():
        who = {"dp": to, "graph": graph}
        at = chunk(jnp.minimum(to, 5))
        send(g1.at[at, :], g1_in.at[dp], d_send.at[0, k], d_recv.at[0, k], who, to <= 5)

    hi, lo = split(sum_a)
    all_cot = feats[1].reshape(NODES, D)
    rows_a = jnp.concatenate([mm(chosen, hi, NT), mm(chosen, lo, NT)], 0).astype(BF)
    m = norm_scale * mm(rows_a, all_cot)
    g2[...] = (m[0:48] + m[48:96]).reshape(3, ROWS, D)
    for k, to in others():
        who = {"dp": to, "graph": graph}
        src = g2.at[jnp.maximum(to - 5, 0)]
        send(src, g2_in.at[dp], d_send.at[1, k], d_recv.at[1, k], who, to >= 5)

    weights = hi.astype(F32).T[W : W + 16], lo.astype(F32).T[W : W + 16]
    m = norm_scale * mm(jnp.concatenate(weights, 0).astype(BF), all_cot)
    bias_out[0:1, 0:D] = (m[0:1] + m[1:2]) + (m[16:17] + m[17:18])
    bias_out[0:1, D:] = jnp.sum(sum_t, axis=0, keepdims=True)
    bias_out[1:8, :] = jnp.zeros((7, D + 128), F32)
    bias_in[dp] = bias_out[...]
    for k, to in others():
        who = {"dp": to, "graph": graph}
        send(bias_out, bias_in.at[dp], d_send.at[2, k], d_recv.at[2, k], who)

    @pl.when(dp <= 5)
    def _():
        g1_in[dp] = g1[chunk(jnp.minimum(dp, 5)), :]

    @pl.when(dp >= 5)
    def _():
        g2_in[dp] = g2[jnp.maximum(dp - 5, 0)]

    for k in range(1, 8):
        arrived(own.at[zat(-k)], a_send.at[k], a_recv.at[k])
    pieces = []
    for kind in range(3):
        x = jnp.concatenate([own[k, :, kind * 128 : (kind + 1) * 128] for k in range(8)], 1)
        pieces += split(x)
    rows = mm(jnp.concatenate(pieces, 0), perm[...], NT).astype(BF)
    m = mm(rows[0:32], w2_ref[...])
    sw = own[0, :, W : W + 1] + own[0, :, W + 1 : W + 2]
    summed = m[0:ROWS] + m[ROWS:] + sw * bias_ref[1:2, :]
    m = mm(rows[32:64], w1_ref[0:D, :], NT) + mm(rows[64:96], w1_ref[D : 2 * D, :], NT)
    out_ref[0] = (nodes_ref[0].astype(F32) + norm_scale * summed).astype(BF)
    grad_ref[0] = cot_ref[0].astype(F32) + (m[0:ROWS] + m[ROWS:])

    from_z = z // 4

    @pl.when(dp <= 5)
    def _():
        for k in range(1, 8):
            arrived(g1_in.at[(dp - k + 8) % 8], d_send.at[0, k], d_recv.at[0, k])
        acc = g1_in[0]
        for k in range(1, 8):
            acc += g1_in[k]
        g1_sum[...] = acc
        for j in range(8):
            g1_out[j, 0:9, :] = g1_sum[9 * j : 9 * j + 9, :]
            g1_out[j, 9:16, :] = jnp.zeros((7, 128), F32)

    for j in range(8):
        elsewhere = jnp.logical_not((z == 4 * c + j // 2) & (c == j % 2))
        send(
            g1_out.at[j],
            g1_last.at[z],
            f_send.at[j],
            f_recv.at[z],
            {"dp": dp, "graph": 8 * quarter + j},
            (dp <= 5) & elsewhere,
        )

    @pl.when((dp <= 5) & (c == from_z))
    def _():
        g1_last[z] = g1_out[(z % 4) * 2 + c]

    for k in range(1, 8):
        arrived(bias_in.at[(dp - k + 8) % 8], d_send.at[2, k], d_recv.at[2, k])
    acc = bias_in[0]
    for k in range(1, 8):
        acc += bias_in[k]
    bias_mine[...] = acc[:, D:]
    bias_last[z] = acc[:, D:]
    for k in range(1, 8):
        send(bias_mine, bias_last.at[z], b_send.at[k], b_recv.at[k], peer(y, zat(k), c))
    bias_one = acc[0:1, 0:D]

    @pl.when(dp > 5)
    def _():
        g1_last[...] = jnp.zeros_like(g1_last)

    gsum_ref[...] = jnp.zeros_like(gsum_ref)

    @pl.when(dp >= 5)
    def _():
        for k in range(1, 8):
            arrived(g2_in.at[(dp - k + 8) % 8], d_send.at[1, k], d_recv.at[1, k])
        acc = g2_in[0]
        for k in range(1, 8):
            acc += g2_in[k]
        gsum_ref[...] = acc

    for k in range(1, 8):
        arrived(bias_last.at[zat(-k)], b_send.at[k], b_recv.at[k])
    for k in range(8):
        here = jnp.logical_not((z == k) & (c == from_z))

        @pl.when((dp <= 5) & here)
        def _():
            arrived(g1_last.at[k], f_send.at[0], f_recv.at[k])

    g = jnp.concatenate([g1_last[k] for k in range(8)], 1)
    b = jnp.concatenate([bias_last[k] for k in range(8)], 1)
    g = jnp.concatenate(split(jnp.concatenate([g, b, jnp.zeros_like(b)], 0)), 0)
    m = mm(g, perm[...], NT)
    m = m[0:32] + m[32:64]
    gsum_ref[0:9, :] += m[0:9]
    gsum_ref[9:10, :] = m[16:17]
    gsum_ref[10:11, :] = bias_one

    for copy, when in pending:
        if when is None:
            copy.wait_send()
        else:
            pl.when(when)(copy.wait_send)


def shards(
    nodes,
    cotangent,
    sources,
    targets,
    edge_weight,
    w_first,
    w_second,
    biases,
    master,
    moment_first,
    moment_second,
    bias_first,
    bias_second,
):
    norm_scale = 1.0 / math.sqrt(sources.shape[1] / nodes.shape[1])
    groups = lax.axis_size("dp")

    def kernel(*refs):
        layer_kernel(norm_scale, *refs)

    vmem = pl.BlockSpec(memory_space=pltpu.VMEM)
    dma = pltpu.SemaphoreType.DMA
    node_out, node_grad, gsum = pl.pallas_call(
        kernel,
        out_shape=(
            jax.ShapeDtypeStruct((1, ROWS, D), BF),
            jax.ShapeDtypeStruct((1, ROWS, D), F32),
            jax.ShapeDtypeStruct((ROWS, D), F32),
        ),
        in_specs=[pl.BlockSpec(memory_space=pltpu.HBM)] * 8,
        out_specs=(vmem, vmem, vmem),
        scratch_shapes=[
            pltpu.VMEM((1, ROWS, D), BF),
            pltpu.VMEM((1, ROWS, D), BF),
            pltpu.VMEM((1, EDGE), jnp.int32),
            pltpu.VMEM((1, EDGE), jnp.int32),
            pltpu.VMEM((1, EDGE), F32),
            pltpu.VMEM((2 * D, D), BF),
            pltpu.VMEM((D, D), BF),
            pltpu.VMEM((2, D), F32),
            pltpu.VMEM((2, 2, 2, 128, D), BF),
            pltpu.VMEM((NZ, 24, 128), F32),
            pltpu.VMEM((D, NZ * 128), BF),
            pltpu.VMEM((NZ, 4, ROWS, 128), BF),
            pltpu.VMEM((4, NODES, 128), BF),
            pltpu.VMEM((W, NODES), BF),
            pltpu.VMEM((3 * W, NODES), BF),
            pltpu.VMEM((NODES, EDGE), BF),
            pltpu.VMEM((NODES, EDGE), BF),
            pltpu.VMEM((8, EDGE), F32),
            pltpu.VMEM((2, 256, 384), F32),
            pltpu.VMEM((256, 384), F32),
            pltpu.VMEM((256, 384), BF),
            pltpu.VMEM((256, 384), BF),
            pltpu.VMEM((2, 256, 384), F32),
            pltpu.VMEM((NZ, ROWS, 384), F32),
            pltpu.VMEM((D, NODES), BF),
            pltpu.VMEM((6 * 288, 128), F32),
            pltpu.VMEM((8, 72, 128), F32),
            pltpu.VMEM((72, 128), F32),
            pltpu.VMEM((8, ROWS, 128), F32),
            pltpu.VMEM((NZ, ROWS, 128), F32),
            pltpu.VMEM((3, ROWS, D), F32),
            pltpu.VMEM((8, ROWS, D), F32),
            pltpu.VMEM((8, D + 128), F32),
            pltpu.VMEM((8, 8, D + 128), F32),
            pltpu.VMEM((8, 128), F32),
            pltpu.VMEM((NZ, 8, 128), F32),
            dma((2,)),
            dma((2,)),
            dma((2, 4, 2)),
            dma((2, 4, 2)),
            dma((8, 2)),
            dma((8, 2)),
            dma((8,)),
            dma((8,)),
            dma((4, 8)),
            dma((4, 8)),
            dma((3,)),
            dma((3,)),
            dma((8,)),
            dma((8,)),
            dma((3, 8)),
            dma((3, 8)),
            dma((8,)),
            dma((8,)),
            dma((8,)),
            dma((8,)),
            dma((8,)),
        ],
        compiler_params=pltpu.CompilerParams(
            collective_id=0, has_side_effects=True, vmem_limit_bytes=63 * 1024 * 1024
        ),
        name="layer",
    )(nodes, cotangent, sources, targets, edge_weight, w_first, w_second, biases)

    grads = gsum[0:9].reshape(-1) / groups
    bias_grads = gsum[9:11] / groups
    new_master, new_first, new_second = adam_update(master, moment_first, moment_second, grads)
    new_biases, new_bias_first, new_bias_second = adam_update(
        biases, bias_first, bias_second, bias_grads
    )
    return (
        node_out,
        node_grad,
        new_master,
        new_first,
        new_second,
        new_biases,
        new_bias_first,
        new_bias_second,
    )


def solution(mesh):
    placed = (
        P("dp", "graph", None),
        P("dp", "graph", None),
        P("dp", "graph"),
        P("dp", "graph"),
        P("dp", "graph"),
        P(),
        P(),
        P(),
        P(("dp", "graph")),
        P(("dp", "graph")),
        P(("dp", "graph")),
        P(),
        P(),
    )
    return jax.shard_map(
        shards,
        mesh=mesh,
        in_specs=placed,
        out_specs=(
            P("dp", "graph", None),
            P("dp", "graph", None),
            P(("dp", "graph")),
            P(("dp", "graph")),
            P(("dp", "graph")),
            P(),
            P(),
            P(),
        ),
        check_vma=False,
    )
```

```python
import math

import jax
import jax.numpy as jnp
from jax import lax
from jax.experimental import pallas as pl
from jax.experimental.pallas import tpu as pltpu
from jax.sharding import PartitionSpec as P

STEP = 10


beta_one = 0.9
beta_two = 0.999
epsilon = 1e-08
learn_rate = 0.001

D = 768
ROWS = 16
EDGE = 1024
NZ = 8
ORDER = (4, 5, 3, 6, 2, 7, 1)
W = 112
NODES = 512
BF = jnp.bfloat16
F32 = jnp.float32
NN = (((1,), (0,)), ((), ()))
NT = (((1,), (1,)), ((), ()))
TN = (((0,), (0,)), ((), ()))


def mm(a, b, dims=NN):
    return lax.dot_general(a, b, dims, preferred_element_type=F32)


def split(x):
    hi = x.astype(BF)
    return hi, (x - hi.astype(F32)).astype(BF)


def adam_update(param, first, second, grads):
    new_first = beta_one * first + (1.0 - beta_one) * grads
    new_second = beta_two * second + (1.0 - beta_two) * grads * grads
    ratio = (
        new_first
        / (1.0 - beta_one**STEP)
        / (jnp.sqrt(new_second / (1.0 - beta_two**STEP)) + epsilon)
    )
    return (param - learn_rate * ratio, new_first, new_second)


def column_of(z, i):
    owner = ((i % 36) // 18) * 16 + z * 2 + ((i % 18) // 9)
    h = (5 + i // 36) * 288 + owner * 9 + i % 9 - 2 * D
    return jnp.where((i < 108) & (h >= 0), h, -1)


def layer_kernel(
    norm_scale,
    nodes_hbm,
    cot_hbm,
    src_hbm,
    tgt_hbm,
    weight_hbm,
    w1_hbm,
    w2_hbm,
    bias_hbm,
    out_ref,
    grad_ref,
    gsum_ref,
    bsum_ref,
    nodes_ref,
    cot_ref,
    src_ref,
    tgt_ref,
    weight_ref,
    w1_ref,
    w2_ref,
    bias_ref,
    feats,
    edges,
    perm,
    prod_out,
    prod,
    psrc,
    ptgt,
    onehot_s,
    onehot_t,
    row,
    part,
    part_in,
    half_out,
    half_in,
    total,
    own,
    flip,
    g1,
    g1_half,
    g1_in,
    g1_sum,
    g1_out,
    g1_last,
    g2,
    g2_in,
    g2_sum,
    bias_out,
    bias_in,
    bias_mine,
    bias_last,
    y_send,
    y_recv,
    z_send,
    z_recv,
    c_send,
    c_recv,
    e_send,
    e_recv,
    p_send,
    p_recv,
    r_send,
    r_recv,
    a_send,
    a_recv,
    d_send,
    d_recv,
    f_send,
    f_recv,
    b_send,
    b_recv,
    l_sem,
):
    dp = lax.axis_index("dp")
    graph = lax.axis_index("graph")
    y = graph // 16
    z = (graph // 2) % 8
    c = graph % 2
    quarter = y * 2 + c

    def peer(py, pz, pc):
        return {"dp": dp, "graph": py * 16 + pz * 2 + pc}

    def zat(k):
        return (z + k + 8) % 8

    y_peer = peer(1 - y, z, c)
    c_peer = peer(y, z, 1 - c)
    right = peer(y, zat(1), c)
    left = peer(y, zat(-1), c)

    loads = [
        pltpu.make_async_copy(src, dst, l_sem.at[i])
        for i, (src, dst) in enumerate(
            [
                (nodes_hbm, nodes_ref),
                (cot_hbm, cot_ref),
                (src_hbm, src_ref),
                (tgt_hbm, tgt_ref),
                (weight_hbm, weight_ref),
                (bias_hbm, bias_ref),
                (w1_hbm, w1_ref),
                (w2_hbm, w2_ref),
            ]
        )
    ]
    for load in loads:
        load.start()

    barrier = pltpu.get_barrier_semaphore()
    greet = [y_peer, c_peer]
    for k in range(1, 8):
        greet += [peer(y, zat(k), c), peer(y, zat(k), 1 - c), {"dp": (dp + k) % 8, "graph": graph}]
    for who in greet:
        pl.semaphore_signal(barrier, inc=1, device_id=who, device_id_type=pl.DeviceIdType.MESH)

    def remote(src, dst, send, recv, who):
        return pltpu.make_async_remote_copy(
            src_ref=src,
            dst_ref=dst,
            send_sem=send,
            recv_sem=recv,
            device_id=who,
            device_id_type=pl.DeviceIdType.MESH,
        )

    pending = []

    def send(src, dst, ssem, rsem, who, when=None):
        copy = remote(src, dst, ssem, rsem, who)
        if when is None:
            copy.start()
        else:
            pl.when(when)(copy.start)
        pending.append((copy, when))

    def arrived(dst, ssem, rsem):
        remote(dst, dst, ssem, rsem, right).wait_recv()

    at_h = lax.broadcasted_iota(jnp.int32, (D, 128), 0)
    for k in range(8):
        place_of = column_of(k, lax.broadcasted_iota(jnp.int32, (1, 128), 1))
        perm[:, k * 128 : (k + 1) * 128] = jnp.where(at_h == place_of, 1.0, 0.0).astype(BF)

    for load in loads[0:5]:
        load.wait()
    zrow = pl.multiple_of(z * ROWS, ROWS)
    feats[0, c, y, pl.ds(zrow, ROWS), :] = nodes_ref[0]
    feats[1, c, y, pl.ds(zrow, ROWS), :] = cot_ref[0]

    def place(n):
        ny, nz, nc, nr = n // 256, (n // 32) % 8, (n // 16) % 2, n % 16
        return nc * 256 + ny * 128 + nz * 16 + nr

    for j in range(8):
        lanes = slice(j * 128, (j + 1) * 128)
        ends = place(src_ref[0:1, lanes]) + NODES * place(tgt_ref[0:1, lanes])
        edges[z, j : j + 1, :] = ends.astype(F32)
        edges[z, 8 + j : 9 + j, :] = weight_ref[0:1, lanes]

    for load in loads[5:8]:
        load.wait()
    from_s = mm(nodes_ref[0], w1_ref[0:D, :]).astype(BF)
    from_t = split(mm(nodes_ref[0], w1_ref[D : 2 * D, :]))
    from_c = (norm_scale * mm(cot_ref[0], w2_ref[...], NT)).astype(BF)
    stack = jnp.concatenate([from_s, from_t[0], from_t[1], from_c], 0)
    spread = mm(stack, perm[...])
    for k in range(8):
        for kind in range(4):
            rows = slice(kind * ROWS, (kind + 1) * ROWS)
            prod_out[k, kind] = spread[rows, k * 128 : (k + 1) * 128].astype(BF)

    pl.semaphore_wait(barrier, len(greet))

    def zbase(pc, py, pz):
        return pl.multiple_of(pc * 256 + py * 128 + pz * ROWS, ROWS)

    def products(pc, py, pz):
        return prod.at[:, pl.ds(zbase(pc, py, pz), ROWS), :]

    for kind in range(2):
        mine = feats.at[kind, c, y, pl.ds(zrow, ROWS), :]
        send(mine, mine, y_send.at[kind], y_recv.at[kind], y_peer)
    for k in ORDER:
        send(edges.at[z], edges.at[z], e_send.at[k], e_recv.at[k], peer(y, zat(k), c))
    for k in ORDER:
        to = peer(y, zat(k), c)
        send(prod_out.at[zat(k)], products(c, y, z), p_send.at[0, k], p_recv.at[0, k], to)
    prod[:, pl.ds(zbase(c, y, z), ROWS), :] = prod_out[z]

    def slot(kind, at):
        return feats.at[kind, c, :, pl.ds(pl.multiple_of(at * ROWS, ROWS), ROWS), :]

    def other_slot(kind, at):
        return feats.at[kind, 1 - c, :, pl.ds(pl.multiple_of(at * ROWS, ROWS), ROWS), :]

    def to_right(kind, k):
        ref = slot(kind, zat(-k))
        send(ref, ref, z_send.at[0, k, kind], z_recv.at[0, k, kind], right)

    def to_left(kind, k):
        ref = slot(kind, zat(k))
        send(ref, ref, z_send.at[1, k, kind], z_recv.at[1, k, kind], left)

    def to_core(kind, k):
        ref = slot(kind, zat(k))
        send(ref, ref, c_send.at[k % 8, kind], c_recv.at[k % 8, kind], c_peer)

    def ring(k):
        for kind in range(2):
            arrived(slot(kind, zat(-k)), z_send.at[0, k - 1, kind], z_recv.at[0, k - 1, kind])
            if k < 4:
                to_right(kind, k)
            to_core(kind, -k)
            if k < 4:
                arrived(slot(kind, zat(k)), z_send.at[1, k - 1, kind], z_recv.at[1, k - 1, kind])
                if k < 3:
                    to_left(kind, k)
                to_core(kind, k)

    pick = lax.broadcasted_iota(jnp.int32, (W, D), 1) == column_of(
        z, lax.broadcasted_iota(jnp.int32, (W, 1), 0)
    )
    b0 = jnp.sum(jnp.where(pick, bias_ref[0:1, :], 0.0), axis=1, keepdims=True)
    part[...] = jnp.zeros_like(part)

    def build(i):
        ids = lax.broadcasted_iota(jnp.int32, (NODES, 128), 0)
        for j in range(8):
            lanes = slice(j * 128, (j + 1) * 128)
            ends = edges[i, j : j + 1, :].astype(jnp.int32)
            onehot_s[i, :, lanes] = jnp.where(ids == (ends & (NODES - 1)), 1.0, 0.0).astype(BF)
            onehot_t[i, :, lanes] = jnp.where(ids == (ends >> 9), 1.0, 0.0).astype(BF)
            row[i, 0:1, lanes] = edges[i, 8 + j : 9 + j, :]

    def onward(k):
        ref = products(c, y, zat(-k))
        if k:
            arrived(ref, p_send.at[0, k], p_recv.at[0, k])
        send(ref, ref, p_send.at[1, k], p_recv.at[1, k], y_peer)
        send(ref, ref, p_send.at[2, k], p_recv.at[2, k], c_peer)

    near = ORDER[::-1]
    onward(0)
    build(z)
    for k in near:
        arrived(edges.at[zat(-k)], e_send.at[k], e_recv.at[k])
        build(zat(-k))
        onward(k)
        if k == near[1]:
            for kind in range(2):
                theirs = feats.at[kind, c, 1 - y, pl.ds(zrow, ROWS), :]
                arrived(theirs, y_send.at[kind], y_recv.at[kind])
                to_right(kind, 0)
                to_left(kind, 0)
                to_core(kind, 0)
    for k in (0,) + near:
        ref = products(c, 1 - y, zat(-k))
        arrived(ref, p_send.at[1, k], p_recv.at[1, k])
        send(ref, ref, p_send.at[3, k], p_recv.at[3, k], c_peer)
    for k in range(8):
        arrived(products(1 - c, y, zat(-k)), p_send.at[2, k], p_recv.at[2, k])
        arrived(products(1 - c, 1 - y, zat(-k)), p_send.at[3, k], p_recv.at[3, k])

    psrc[...] = prod[0].astype(F32).T[0:W].astype(BF)
    for kind in range(3):
        ptgt[kind * W : (kind + 1) * W] = prod[kind + 1].astype(F32).T[0:W].astype(BF)

    def edge_block(i, carry):
        w = row[i, 0:1, :]
        u = mm(psrc[...], onehot_s[i])
        v = mm(ptgt[...], onehot_t[i])
        pre = (u + v[0:W]) + v[W : 2 * W] + b0
        sg = 0.5 * jnp.tanh(0.5 * pre) + 0.5
        act = pre * sg
        dpre = ((v[2 * W : 3 * W] * w) * (sg * (1.0 + pre - act))).astype(BF)
        w_hi, w_lo = split(w)
        rank = lax.broadcasted_iota(jnp.int32, (128 - W, EDGE), 0)
        tail = jnp.where(rank == 0, w_hi.astype(F32), jnp.where(rank == 1, w_lo.astype(F32), 0.0))
        zeros = jnp.zeros((128 - W, EDGE), BF)
        to_t = jnp.concatenate([(act * w).astype(BF), tail.astype(BF), dpre, zeros], 0)
        to_s = jnp.concatenate([dpre, zeros], 0)
        at = mm(onehot_t[i], to_t, NT)
        s = mm(onehot_s[i], to_s, NT)
        for h in range(2):
            rows = slice(h * 256, (h + 1) * 256)
            part[h, :, 0:128] += at[rows, 0:128]
            part[h, :, 256:384] += at[rows, 128:256]
            part[h, :, 128:256] += s[rows, :]
        return carry

    for k in range(4):
        lax.fori_loop(2 * k, 2 * k + 2, edge_block, 0)
        if k < 3:
            ring(k + 1)

    send(part.at[1 - c], part_in, r_send.at[0], r_recv.at[0], c_peer)
    arrived(part_in, r_send.at[0], r_recv.at[0])
    half_out[...] = (part[c] + part_in[...]).astype(BF)
    send(half_out, half_in, r_send.at[1], r_recv.at[1], y_peer)
    ring(4)

    for kind in range(2):
        for k in range(8):
            arrived(other_slot(kind, zat(k)), c_send.at[k, kind], c_recv.at[k, kind])
    flip[...] = feats[0].reshape(NODES, D).astype(F32).T.astype(BF)
    lane = lax.broadcasted_iota(jnp.int32, (48, 128), 1)
    mine = lax.broadcasted_iota(jnp.int32, (48, 128), 0)
    wanted = jnp.where(mine % 16 < 9, (mine // 16) * 36 + quarter * 9 + mine % 16, -1)
    chosen = jnp.where(lane == wanted, 1.0, 0.0).astype(BF)

    arrived(half_in, r_send.at[1], r_recv.at[1])
    total[c] = half_out[...].astype(F32) + half_in[...].astype(F32)
    send(total.at[c], total.at[c], r_send.at[2], r_recv.at[2], c_peer)

    own[z] = total[c, pl.ds(pl.multiple_of(y * 128 + z * ROWS, ROWS), ROWS), :]
    for k in range(1, 8):
        rows = pl.ds(pl.multiple_of(y * 128 + zat(k) * ROWS, ROWS), ROWS)
        send(total.at[c, rows, :], own.at[z], a_send.at[k], a_recv.at[k], peer(y, zat(k), c))

    arrived(total.at[1 - c], r_send.at[2], r_recv.at[2])

    def sums(kind):
        return total[:, :, kind * 128 : (kind + 1) * 128].reshape(NODES, 128)

    sum_a, sum_s, sum_t = sums(0), sums(1), sums(2)
    for kind, x in enumerate((sum_s, sum_t)):
        m = mm(flip[...], jnp.concatenate(split(x), 1))
        g1[kind * D : (kind + 1) * D, :] = m[:, 0:128] + m[:, 128:256]
    g1[2 * D :, :] = jnp.zeros((6 * 288 - 2 * D, 128), F32)

    def chunk(to):
        return pl.ds(pl.multiple_of(to * 288 + quarter * 72, 8), 72)

    for d in range(6):
        rows = jnp.concatenate([g1[chunk(d), :], jnp.zeros((8, 128), F32)], 0)
        g1_half[d] = rows.astype(BF)

    def others():
        return [(k, (dp + k) % 8) for k in range(1, 8)]

    for k, to in others():
        who = {"dp": to, "graph": graph}
        src = g1_half.at[jnp.minimum(to, 5)]
        send(src, g1_in.at[dp], d_send.at[0, k], d_recv.at[0, k], who, to <= 5)

    hi, lo = split(sum_a)
    all_cot = feats[1].reshape(NODES, D)
    rows_a = jnp.concatenate([mm(chosen, hi, NT), mm(chosen, lo, NT)], 0).astype(BF)
    m = norm_scale * mm(rows_a, all_cot)
    g2[...] = (m[0:48] + m[48:96]).reshape(3, ROWS, D).astype(BF)
    for k, to in others():
        who = {"dp": to, "graph": graph}
        src = g2.at[jnp.maximum(to - 5, 0)]
        send(src, g2_in.at[dp], d_send.at[1, k], d_recv.at[1, k], who, to >= 5)

    weights = hi.astype(F32).T[W : W + 16], lo.astype(F32).T[W : W + 16]
    m = norm_scale * mm(jnp.concatenate(weights, 0).astype(BF), all_cot)
    second = (m[0:1] + m[1:2]) + (m[16:17] + m[17:18])
    for k in range(6):
        bias_out[k : k + 1, :] = second[:, k * 128 : (k + 1) * 128]
    bias_out[6:7, :] = jnp.sum(sum_t, axis=0, keepdims=True)
    bias_out[7:8, :] = jnp.zeros((1, 128), F32)
    bias_in[dp] = bias_out[...]
    for k, to in others():
        who = {"dp": to, "graph": graph}
        send(bias_out, bias_in.at[dp], d_send.at[2, k], d_recv.at[2, k], who)

    @pl.when(dp <= 5)
    def _():
        g1_in[dp] = g1_half[jnp.minimum(dp, 5)]

    @pl.when(dp >= 5)
    def _():
        g2_in[dp] = g2[jnp.maximum(dp - 5, 0)]

    for k in range(1, 8):
        arrived(own.at[zat(-k)], a_send.at[k], a_recv.at[k])
    pieces = []
    for kind in range(3):
        x = jnp.concatenate([own[k, :, kind * 128 : (kind + 1) * 128] for k in range(8)], 1)
        pieces += split(x)
    rows = mm(jnp.concatenate(pieces, 0), perm[...], NT).astype(BF)
    m = mm(rows[0:32], w2_ref[...])
    sw = own[0, :, W : W + 1] + own[0, :, W + 1 : W + 2]
    summed = m[0:ROWS] + m[ROWS:] + sw * bias_ref[1:2, :]
    m = mm(rows[32:64], w1_ref[0:D, :], NT) + mm(rows[64:96], w1_ref[D : 2 * D, :], NT)
    out_ref[0] = (nodes_ref[0].astype(F32) + norm_scale * summed).astype(BF)
    grad_ref[0] = cot_ref[0].astype(F32) + (m[0:ROWS] + m[ROWS:])

    from_z = z // 4

    @pl.when(dp <= 5)
    def _():
        for k in range(1, 8):
            arrived(g1_in.at[(dp - k + 8) % 8], d_send.at[0, k], d_recv.at[0, k])
        acc = g1_in[0].astype(F32)
        for k in range(1, 8):
            acc += g1_in[k].astype(F32)
        g1_sum[...] = acc
        for j in range(8):
            g1_out[j, 0:9, :] = g1_sum[9 * j : 9 * j + 9, :]
            g1_out[j, 9:16, :] = jnp.zeros((7, 128), F32)

    for j in range(8):
        elsewhere = jnp.logical_not((z == 4 * c + j // 2) & (c == j % 2))
        send(
            g1_out.at[j],
            g1_last.at[z],
            f_send.at[j],
            f_recv.at[z],
            {"dp": dp, "graph": 8 * quarter + j},
            (dp <= 5) & elsewhere,
        )

    @pl.when((dp <= 5) & (c == from_z))
    def _():
        g1_last[z] = g1_out[(z % 4) * 2 + c]

    for k in range(1, 8):
        arrived(bias_in.at[(dp - k + 8) % 8], d_send.at[2, k], d_recv.at[2, k])
    acc = bias_in[0]
    for k in range(1, 8):
        acc += bias_in[k]
    bias_mine[...] = acc
    bias_last[z] = acc
    for k in range(1, 8):
        send(bias_mine, bias_last.at[z], b_send.at[k], b_recv.at[k], peer(y, zat(k), c))
    for k in range(6):
        bsum_ref[1:2, k * 128 : (k + 1) * 128] = acc[k : k + 1, :]

    @pl.when(dp > 5)
    def _():
        g1_last[...] = jnp.zeros_like(g1_last)

    @pl.when(dp < 5)
    def _():
        g2_sum[...] = jnp.zeros_like(g2_sum)

    @pl.when(dp >= 5)
    def _():
        for k in range(1, 8):
            arrived(g2_in.at[(dp - k + 8) % 8], d_send.at[1, k], d_recv.at[1, k])
        acc = g2_in[0].astype(F32)
        for k in range(1, 8):
            acc += g2_in[k].astype(F32)
        g2_sum[...] = acc

    for k in range(1, 8):
        arrived(bias_last.at[zat(-k)], b_send.at[k], b_recv.at[k])
    for k in range(8):
        here = jnp.logical_not((z == k) & (c == from_z))

        @pl.when((dp <= 5) & here)
        def _():
            arrived(g1_last.at[k], f_send.at[0], f_recv.at[k])

    g = jnp.concatenate([g1_last[k] for k in range(8)], 1)
    b = jnp.concatenate([bias_last[k] for k in range(8)], 1)
    g = jnp.concatenate(split(jnp.concatenate([g, b, jnp.zeros_like(b)], 0)), 0)
    m = mm(g, perm[...], NT)
    m = m[0:32] + m[32:64]
    g = g2_sum[0:9, :] + m[0:9]
    for k in range(6):
        gsum_ref[pl.ds(k, 9, stride=6), :] = g[:, k * 128 : (k + 1) * 128]
    gsum_ref[54:56, :] = jnp.zeros((2, 128), F32)
    bsum_ref[0:1, :] = m[22:23]
    bsum_ref[2:8, :] = jnp.zeros((6, D), F32)

    for copy, when in pending:
        if when is None:
            copy.wait_send()
        else:
            pl.when(when)(copy.wait_send)


def shards(
    nodes,
    cotangent,
    sources,
    targets,
    edge_weight,
    w_first,
    w_second,
    biases,
    master,
    moment_first,
    moment_second,
    bias_first,
    bias_second,
):
    norm_scale = 1.0 / math.sqrt(sources.shape[1] / nodes.shape[1])
    groups = lax.axis_size("dp")

    def kernel(*refs):
        layer_kernel(norm_scale, *refs)

    vmem = pl.BlockSpec(memory_space=pltpu.VMEM)
    dma = pltpu.SemaphoreType.DMA
    node_out, node_grad, gsum, bsum = pl.pallas_call(
        kernel,
        out_shape=(
            jax.ShapeDtypeStruct((1, ROWS, D), BF),
            jax.ShapeDtypeStruct((1, ROWS, D), F32),
            jax.ShapeDtypeStruct((56, 128), F32),
            jax.ShapeDtypeStruct((8, D), F32),
        ),
        in_specs=[pl.BlockSpec(memory_space=pltpu.HBM)] * 8,
        out_specs=(vmem,) * 4,
        scratch_shapes=[
            pltpu.VMEM((1, ROWS, D), BF),
            pltpu.VMEM((1, ROWS, D), BF),
            pltpu.VMEM((1, EDGE), jnp.int32),
            pltpu.VMEM((1, EDGE), jnp.int32),
            pltpu.VMEM((1, EDGE), F32),
            pltpu.VMEM((2 * D, D), BF),
            pltpu.VMEM((D, D), BF),
            pltpu.VMEM((2, D), F32),
            pltpu.VMEM((2, 2, 2, 128, D), BF),
            pltpu.VMEM((NZ, 16, 128), F32),
            pltpu.VMEM((D, NZ * 128), BF),
            pltpu.VMEM((NZ, 4, ROWS, 128), BF),
            pltpu.VMEM((4, NODES, 128), BF),
            pltpu.VMEM((W, NODES), BF),
            pltpu.VMEM((3 * W, NODES), BF),
            pltpu.VMEM((NZ, NODES, EDGE), BF),
            pltpu.VMEM((NZ, NODES, EDGE), BF),
            pltpu.VMEM((NZ, 8, EDGE), F32),
            pltpu.VMEM((2, 256, 384), F32),
            pltpu.VMEM((256, 384), F32),
            pltpu.VMEM((256, 384), BF),
            pltpu.VMEM((256, 384), BF),
            pltpu.VMEM((2, 256, 384), F32),
            pltpu.VMEM((NZ, ROWS, 384), F32),
            pltpu.VMEM((D, NODES), BF),
            pltpu.VMEM((6 * 288, 128), F32),
            pltpu.VMEM((6, 80, 128), BF),
            pltpu.VMEM((8, 80, 128), BF),
            pltpu.VMEM((80, 128), F32),
            pltpu.VMEM((8, ROWS, 128), F32),
            pltpu.VMEM((NZ, ROWS, 128), F32),
            pltpu.VMEM((3, ROWS, D), BF),
            pltpu.VMEM((8, ROWS, D), BF),
            pltpu.VMEM((ROWS, D), F32),
            pltpu.VMEM((8, 128), F32),
            pltpu.VMEM((8, 8, 128), F32),
            pltpu.VMEM((8, 128), F32),
            pltpu.VMEM((NZ, 8, 128), F32),
            dma((2,)),
            dma((2,)),
            dma((2, 4, 2)),
            dma((2, 4, 2)),
            dma((8, 2)),
            dma((8, 2)),
            dma((8,)),
            dma((8,)),
            dma((4, 8)),
            dma((4, 8)),
            dma((3,)),
            dma((3,)),
            dma((8,)),
            dma((8,)),
            dma((3, 8)),
            dma((3, 8)),
            dma((8,)),
            dma((8,)),
            dma((8,)),
            dma((8,)),
            dma((8,)),
        ],
        compiler_params=pltpu.CompilerParams(
            collective_id=0, has_side_effects=True, vmem_limit_bytes=63 * 1024 * 1024
        ),
        name="layer",
    )(nodes, cotangent, sources, targets, edge_weight, w_first, w_second, biases)

    def finish(*refs):
        out, back, grads, bias_grads = refs[0:4]
        refs[10][...] = out[...]
        refs[11][...] = back[...]
        new = adam_update(refs[4][...], refs[5][...], refs[6][...], grads[0:54, :] / groups)
        for ref, value in zip(refs[12:15], new):
            ref[...] = value
        new = adam_update(refs[7][...], refs[8][...], refs[9][...], bias_grads[0:2, :] / groups)
        for ref, value in zip(refs[15:18], new):
            ref[...] = value

    flat = (54, 128)
    done = pl.pallas_call(
        finish,
        out_shape=(
            jax.ShapeDtypeStruct((1, ROWS, D), BF),
            jax.ShapeDtypeStruct((1, ROWS, D), F32),
        )
        + (jax.ShapeDtypeStruct(flat, F32),) * 3
        + (jax.ShapeDtypeStruct((2, D), F32),) * 3,
        name="finish",
    )(
        node_out,
        node_grad,
        gsum,
        bsum,
        master.reshape(flat),
        moment_first.reshape(flat),
        moment_second.reshape(flat),
        biases,
        bias_first,
        bias_second,
    )
    node_out, node_grad = done[0:2]
    new_master, new_first, new_second = [x.reshape(-1) for x in done[2:5]]
    new_biases, new_bias_first, new_bias_second = done[5:8]
    return (
        node_out,
        node_grad,
        new_master,
        new_first,
        new_second,
        new_biases,
        new_bias_first,
        new_bias_second,
    )


def solution(mesh):
    placed = (
        P("dp", "graph", None),
        P("dp", "graph", None),
        P("dp", "graph"),
        P("dp", "graph"),
        P("dp", "graph"),
        P(),
        P(),
        P(),
        P(("dp", "graph")),
        P(("dp", "graph")),
        P(("dp", "graph")),
        P(),
        P(),
    )
    return jax.shard_map(
        shards,
        mesh=mesh,
        in_specs=placed,
        out_specs=(
            P("dp", "graph", None),
            P("dp", "graph", None),
            P(("dp", "graph")),
            P(("dp", "graph")),
            P(("dp", "graph")),
            P(),
            P(),
            P(),
        ),
        check_vma=False,
    )
```

```python
import math

import jax
import jax.numpy as jnp
from jax import lax
from jax.experimental import pallas as pl
from jax.experimental.pallas import tpu as pltpu
from jax.sharding import PartitionSpec as P

STEP = 10


beta_one = 0.9
beta_two = 0.999
epsilon = 1e-08
learn_rate = 0.001

D = 768
ROWS = 16
EDGE = 1024
NZ = 8
ORDER = (4, 5, 3, 6, 2, 7, 1)
W = 112
NODES = 512
BF = jnp.bfloat16
F32 = jnp.float32
NN = (((1,), (0,)), ((), ()))
NT = (((1,), (1,)), ((), ()))
TN = (((0,), (0,)), ((), ()))


def mm(a, b, dims=NN):
    return lax.dot_general(a, b, dims, preferred_element_type=F32)


def split(x):
    hi = x.astype(BF)
    return hi, (x - hi.astype(F32)).astype(BF)


def adam_update(param, first, second, grads):
    new_first = beta_one * first + (1.0 - beta_one) * grads
    new_second = beta_two * second + (1.0 - beta_two) * grads * grads
    ratio = (
        new_first
        / (1.0 - beta_one**STEP)
        / (jnp.sqrt(new_second / (1.0 - beta_two**STEP)) + epsilon)
    )
    return (param - learn_rate * ratio, new_first, new_second)


def column_of(z, i):
    owner = ((i % 36) // 18) * 16 + z * 2 + ((i % 18) // 9)
    h = (5 + i // 36) * 288 + owner * 9 + i % 9 - 2 * D
    return jnp.where((i < 108) & (h >= 0), h, -1)


def layer_kernel(
    norm_scale,
    nodes_hbm,
    cot_hbm,
    src_hbm,
    tgt_hbm,
    weight_hbm,
    w1_hbm,
    w2_hbm,
    bias_hbm,
    out_ref,
    grad_ref,
    gsum_ref,
    bsum_ref,
    nodes_ref,
    cot_ref,
    src_ref,
    tgt_ref,
    weight_ref,
    w1_ref,
    w2_ref,
    bias_ref,
    feats,
    edges,
    perm,
    prod_out,
    prod,
    psrc,
    ptgt,
    onehot_s,
    onehot_t,
    row,
    part,
    part_in,
    half_out,
    half_in,
    nodes_sum,
    total,
    own,
    flip,
    g1,
    g1_half,
    g1_in,
    g1_sum,
    g1_out,
    g1_last,
    g2,
    g2_in,
    g2_sum,
    bias_out,
    bias_in,
    bias_mine,
    bias_last,
    y_send,
    y_recv,
    z_send,
    z_recv,
    c_send,
    c_recv,
    e_send,
    e_recv,
    p_send,
    p_recv,
    r_send,
    r_recv,
    a_send,
    a_recv,
    d_send,
    d_recv,
    f_send,
    f_recv,
    b_send,
    b_recv,
    l_sem,
):
    dp = lax.axis_index("dp")
    graph = lax.axis_index("graph")
    y = graph // 16
    z = (graph // 2) % 8
    c = graph % 2
    quarter = y * 2 + c

    def peer(py, pz, pc):
        return {"dp": dp, "graph": py * 16 + pz * 2 + pc}

    def zat(k):
        return (z + k + 8) % 8

    y_peer = peer(1 - y, z, c)
    c_peer = peer(y, z, 1 - c)
    right = peer(y, zat(1), c)
    left = peer(y, zat(-1), c)

    loads = [
        pltpu.make_async_copy(src, dst, l_sem.at[i])
        for i, (src, dst) in enumerate(
            [
                (nodes_hbm, nodes_ref),
                (cot_hbm, cot_ref),
                (src_hbm, src_ref),
                (tgt_hbm, tgt_ref),
                (weight_hbm, weight_ref),
                (bias_hbm, bias_ref),
                (w1_hbm, w1_ref),
                (w2_hbm, w2_ref),
            ]
        )
    ]
    for load in loads:
        load.start()

    barrier = pltpu.get_barrier_semaphore()
    greet = [y_peer, c_peer]
    for k in range(1, 8):
        greet += [peer(y, zat(k), c), peer(y, zat(k), 1 - c)]
        greet += [{"dp": (dp + k) % 8, "graph": h * 16 + z * 2 + c} for h in range(2)]
    for who in greet:
        pl.semaphore_signal(barrier, inc=1, device_id=who, device_id_type=pl.DeviceIdType.MESH)

    def remote(src, dst, send, recv, who):
        return pltpu.make_async_remote_copy(
            src_ref=src,
            dst_ref=dst,
            send_sem=send,
            recv_sem=recv,
            device_id=who,
            device_id_type=pl.DeviceIdType.MESH,
        )

    pending = []

    def send(src, dst, ssem, rsem, who, when=None):
        copy = remote(src, dst, ssem, rsem, who)
        if when is None:
            copy.start()
        else:
            pl.when(when)(copy.start)
        pending.append((copy, when))

    def arrived(dst, ssem, rsem):
        remote(dst, dst, ssem, rsem, right).wait_recv()

    at_h = lax.broadcasted_iota(jnp.int32, (D, 128), 0)
    for k in range(8):
        place_of = column_of(k, lax.broadcasted_iota(jnp.int32, (1, 128), 1))
        perm[:, k * 128 : (k + 1) * 128] = jnp.where(at_h == place_of, 1.0, 0.0).astype(BF)

    for load in loads[0:5]:
        load.wait()
    zrow = pl.multiple_of(z * ROWS, ROWS)
    feats[0, c, y, pl.ds(zrow, ROWS), :] = nodes_ref[0]
    feats[1, c, y, pl.ds(zrow, ROWS), :] = cot_ref[0]

    def place(n):
        ny, nz, nc, nr = n // 256, (n // 32) % 8, (n // 16) % 2, n % 16
        return nc * 256 + ny * 128 + nz * 16 + nr

    for j in range(8):
        lanes = slice(j * 128, (j + 1) * 128)
        ends = place(src_ref[0:1, lanes]) + NODES * place(tgt_ref[0:1, lanes])
        edges[z, j : j + 1, :] = ends.astype(F32)
        edges[z, 8 + j : 9 + j, :] = weight_ref[0:1, lanes]

    for load in loads[5:8]:
        load.wait()
    from_s = mm(nodes_ref[0], w1_ref[0:D, :]).astype(BF)
    from_t = split(mm(nodes_ref[0], w1_ref[D : 2 * D, :]))
    from_c = (norm_scale * mm(cot_ref[0], w2_ref[...], NT)).astype(BF)
    stack = jnp.concatenate([from_s, from_t[0], from_t[1], from_c], 0)
    spread = mm(stack, perm[...])
    for k in range(8):
        for kind in range(4):
            rows = slice(kind * ROWS, (kind + 1) * ROWS)
            prod_out[k, kind] = spread[rows, k * 128 : (k + 1) * 128].astype(BF)

    pl.semaphore_wait(barrier, len(greet))

    def zbase(pc, py, pz):
        return pl.multiple_of(pc * 256 + py * 128 + pz * ROWS, ROWS)

    def products(pc, py, pz):
        return prod.at[:, pl.ds(zbase(pc, py, pz), ROWS), :]

    for kind in range(2):
        mine = feats.at[kind, c, y, pl.ds(zrow, ROWS), :]
        send(mine, mine, y_send.at[kind], y_recv.at[kind], y_peer)
    for k in ORDER:
        to = peer(y, zat(k), c)
        send(prod_out.at[zat(k)], products(c, y, z), p_send.at[0, k], p_recv.at[0, k], to)
    for k in ORDER:
        send(edges.at[z], edges.at[z], e_send.at[k], e_recv.at[k], peer(y, zat(k), c))
    prod[:, pl.ds(zbase(c, y, z), ROWS), :] = prod_out[z]

    def slot(kind, at):
        return feats.at[kind, c, :, pl.ds(pl.multiple_of(at * ROWS, ROWS), ROWS), :]

    def other_slot(kind, at):
        return feats.at[kind, 1 - c, :, pl.ds(pl.multiple_of(at * ROWS, ROWS), ROWS), :]

    def to_right(kind, k):
        ref = slot(kind, zat(-k))
        send(ref, ref, z_send.at[0, k, kind], z_recv.at[0, k, kind], right)

    def to_left(kind, k):
        ref = slot(kind, zat(k))
        send(ref, ref, z_send.at[1, k, kind], z_recv.at[1, k, kind], left)

    def to_core(kind, k):
        ref = slot(kind, zat(k))
        send(ref, ref, c_send.at[k % 8, kind], c_recv.at[k % 8, kind], c_peer)

    def ring(k):
        for kind in range(2):
            arrived(slot(kind, zat(-k)), z_send.at[0, k - 1, kind], z_recv.at[0, k - 1, kind])
            if k < 4:
                to_right(kind, k)
            to_core(kind, -k)
            if k < 4:
                arrived(slot(kind, zat(k)), z_send.at[1, k - 1, kind], z_recv.at[1, k - 1, kind])
                if k < 3:
                    to_left(kind, k)
                to_core(kind, k)

    pick = lax.broadcasted_iota(jnp.int32, (W, D), 1) == column_of(
        z, lax.broadcasted_iota(jnp.int32, (W, 1), 0)
    )
    b0 = jnp.sum(jnp.where(pick, bias_ref[0:1, :], 0.0), axis=1, keepdims=True)
    part[...] = jnp.zeros_like(part)

    def build(i):
        ids = lax.broadcasted_iota(jnp.int32, (NODES, 128), 0)
        for j in range(8):
            lanes = slice(j * 128, (j + 1) * 128)
            ends = edges[i, j : j + 1, :].astype(jnp.int32)
            onehot_s[i, :, lanes] = jnp.where(ids == (ends & (NODES - 1)), 1.0, 0.0).astype(BF)
            onehot_t[i, :, lanes] = jnp.where(ids == (ends >> 9), 1.0, 0.0).astype(BF)
            row[i, 0:1, lanes] = edges[i, 8 + j : 9 + j, :]

    def onward(k):
        ref = products(c, y, zat(-k))
        if k:
            arrived(ref, p_send.at[0, k], p_recv.at[0, k])
        send(ref, ref, p_send.at[1, k], p_recv.at[1, k], y_peer)
        send(ref, ref, p_send.at[2, k], p_recv.at[2, k], c_peer)

    near = ORDER[::-1]
    onward(0)
    build(z)
    for k in near:
        onward(k)
        if k == near[1]:
            for kind in range(2):
                theirs = feats.at[kind, c, 1 - y, pl.ds(zrow, ROWS), :]
                arrived(theirs, y_send.at[kind], y_recv.at[kind])
                to_right(kind, 0)
                to_left(kind, 0)
                to_core(kind, 0)
    for k in near:
        arrived(edges.at[zat(-k)], e_send.at[k], e_recv.at[k])
        build(zat(-k))
    for k in (0,) + near:
        ref = products(c, 1 - y, zat(-k))
        arrived(ref, p_send.at[1, k], p_recv.at[1, k])
        send(ref, ref, p_send.at[3, k], p_recv.at[3, k], c_peer)
    for k in range(8):
        arrived(products(1 - c, y, zat(-k)), p_send.at[2, k], p_recv.at[2, k])
        arrived(products(1 - c, 1 - y, zat(-k)), p_send.at[3, k], p_recv.at[3, k])

    psrc[...] = prod[0].astype(F32).T[0:W].astype(BF)
    for kind in range(3):
        ptgt[kind * W : (kind + 1) * W] = prod[kind + 1].astype(F32).T[0:W].astype(BF)

    def edge_block(i, carry):
        w = row[i, 0:1, :]
        u = mm(psrc[...], onehot_s[i])
        v = mm(ptgt[...], onehot_t[i])
        pre = (u + v[0:W]) + v[W : 2 * W] + b0
        sg = 0.5 * jnp.tanh(0.5 * pre) + 0.5
        act = pre * sg
        dpre = ((v[2 * W : 3 * W] * w) * (sg * (1.0 + pre - act))).astype(BF)
        w_hi, w_lo = split(w)
        rank = lax.broadcasted_iota(jnp.int32, (128 - W, EDGE), 0)
        tail = jnp.where(rank == 0, w_hi.astype(F32), jnp.where(rank == 1, w_lo.astype(F32), 0.0))
        zeros = jnp.zeros((128 - W, EDGE), BF)
        to_t = jnp.concatenate([(act * w).astype(BF), tail.astype(BF), dpre, zeros], 0)
        to_s = jnp.concatenate([dpre, zeros], 0)
        at = mm(onehot_t[i], to_t, NT)
        s = mm(onehot_s[i], to_s, NT)
        for h in range(2):
            rows = slice(h * 256, (h + 1) * 256)
            part[h, :, 0:128] += at[rows, 0:128]
            part[h, :, 256:384] += at[rows, 128:256]
            part[h, :, 128:256] += s[rows, :]
        return carry

    for k in range(4):
        lax.fori_loop(2 * k, 2 * k + 2, edge_block, 0, unroll=True)
        if k < 3:
            ring(k + 1)

    send(part, part_in, r_send.at[0], r_recv.at[0], c_peer)
    ring(4)

    for kind in range(2):
        for k in range(8):
            arrived(other_slot(kind, zat(k)), c_send.at[k, kind], c_recv.at[k, kind])
    flip[...] = feats[0].reshape(NODES, D).astype(F32).T.astype(BF)
    lane = lax.broadcasted_iota(jnp.int32, (96, 128), 1)
    mine = lax.broadcasted_iota(jnp.int32, (96, 128), 0)
    of_y = (mine // 48) * 18 + c * 9
    wanted = jnp.where(mine % 16 < 9, (mine % 48 // 16) * 36 + of_y + mine % 16, -1)
    chosen = jnp.where(lane == wanted, 1.0, 0.0).astype(BF)

    arrived(part_in, r_send.at[0], r_recv.at[0])
    total[...] = part[...] + part_in[...]
    half_out[...] = total[c, pl.ds(pl.multiple_of((1 - y) * 128, 128), 128), :].astype(BF)
    send(half_out, half_in, r_send.at[1], r_recv.at[1], y_peer)

    def sums(kind):
        return total[:, :, kind * 128 : (kind + 1) * 128].reshape(NODES, 128)

    sum_a, sum_s, sum_t = sums(0), sums(1), sums(2)
    for kind, x in enumerate((sum_s, sum_t)):
        m = mm(flip[...], jnp.concatenate(split(x), 1))
        g1[kind * D : (kind + 1) * D, :] = m[:, 0:128] + m[:, 128:256]
    g1[2 * D :, :] = jnp.zeros((6 * 288 - 2 * D, 128), F32)

    for h in range(2):
        for d in range(6):
            at = pl.ds(pl.multiple_of(d * 288 + h * 144 + c * 72, 8), 72)
            rows = jnp.concatenate([g1[at, :], jnp.zeros((8, 128), F32)], 0)
            g1_half[h, d] = rows.astype(BF)

    others = []
    for k in range(8):
        for h in range(2):
            if k or h:
                to, ty = (dp + k) % 8, (y + h) % 2
                others.append((k, h, to, ty, {"dp": to, "graph": ty * 16 + z * 2 + c}))

    me = dp * 2 + y
    for k, h, to, ty, who in others:
        src = g1_half.at[ty, jnp.minimum(to, 5)]
        send(src, g1_in.at[me], d_send.at[0, k, h], d_recv.at[0, k, h], who, to <= 5)

    arrived(half_in, r_send.at[1], r_recv.at[1])
    nodes_sum[...] = total[c, pl.ds(pl.multiple_of(y * 128, 128), 128), :] + half_in[...].astype(F32)
    own[z] = nodes_sum[pl.ds(zrow, ROWS), :]
    for k in range(1, 8):
        rows = pl.ds(pl.multiple_of(zat(k) * ROWS, ROWS), ROWS)
        send(nodes_sum.at[rows, :], own.at[z], a_send.at[k], a_recv.at[k], peer(y, zat(k), c))

    hi, lo = split(sum_a)
    all_cot = feats[1].reshape(NODES, D)
    rows_a = jnp.concatenate([mm(chosen, hi, NT), mm(chosen, lo, NT)], 0).astype(BF)
    m = norm_scale * mm(rows_a, all_cot)
    g2[...] = (m[0:96] + m[96:192]).reshape(2, 3, ROWS, D).astype(BF)
    for k, h, to, ty, who in others:
        src = g2.at[ty, jnp.maximum(to - 5, 0)]
        send(src, g2_in.at[me], d_send.at[1, k, h], d_recv.at[1, k, h], who, to >= 5)

    weights = hi.astype(F32).T[W : W + 16], lo.astype(F32).T[W : W + 16]
    m = norm_scale * mm(jnp.concatenate(weights, 0).astype(BF), all_cot)
    second = (m[0:1] + m[1:2]) + (m[16:17] + m[17:18])
    for k in range(6):
        bias_out[k : k + 1, :] = second[:, k * 128 : (k + 1) * 128]
    bias_out[6:7, :] = jnp.sum(sum_t, axis=0, keepdims=True)
    bias_out[7:8, :] = jnp.zeros((1, 128), F32)
    bias_in[me] = bias_out[...]
    for k, h, to, ty, who in others:
        send(bias_out, bias_in.at[me], d_send.at[2, k, h], d_recv.at[2, k, h], who)

    @pl.when(dp <= 5)
    def _():
        g1_in[me] = g1_half[y, jnp.minimum(dp, 5)]

    @pl.when(dp >= 5)
    def _():
        g2_in[me] = g2[y, jnp.maximum(dp - 5, 0)]

    def gathered(ref, stage):
        for k, h, to, ty, who in others:
            at = ((dp - k + 8) % 8) * 2 + (y + h) % 2
            arrived(ref.at[at], d_send.at[stage, k, h], d_recv.at[stage, k, h])
        acc = ref[0].astype(F32)
        for k in range(1, 16):
            acc += ref[k].astype(F32)
        return acc

    from_z = z // 4

    @pl.when(dp <= 5)
    def _():
        acc = gathered(g1_in, 0)
        g1_sum[...] = acc
        for j in range(8):
            g1_out[j, 0:9, :] = g1_sum[9 * j : 9 * j + 9, :]
            g1_out[j, 9:16, :] = jnp.zeros((7, 128), F32)

    for j in range(8):
        elsewhere = jnp.logical_not((z == 4 * c + j // 2) & (c == j % 2))
        send(
            g1_out.at[j],
            g1_last.at[z],
            f_send.at[j],
            f_recv.at[z],
            {"dp": dp, "graph": 8 * quarter + j},
            (dp <= 5) & elsewhere,
        )

    @pl.when((dp <= 5) & (c == from_z))
    def _():
        g1_last[z] = g1_out[(z % 4) * 2 + c]

    acc = gathered(bias_in, 2)
    bias_mine[...] = acc
    bias_last[z] = acc
    for k in range(1, 8):
        send(bias_mine, bias_last.at[z], b_send.at[k], b_recv.at[k], peer(y, zat(k), c))
    for k in range(6):
        bsum_ref[1:2, k * 128 : (k + 1) * 128] = acc[k : k + 1, :]

    for k in range(1, 8):
        arrived(own.at[zat(-k)], a_send.at[k], a_recv.at[k])
    pieces = []
    for kind in range(3):
        x = jnp.concatenate([own[k, :, kind * 128 : (kind + 1) * 128] for k in range(8)], 1)
        pieces += split(x)
    rows = mm(jnp.concatenate(pieces, 0), perm[...], NT).astype(BF)
    m = mm(rows[0:32], w2_ref[...])
    sw = own[0, :, W : W + 1] + own[0, :, W + 1 : W + 2]
    summed = m[0:ROWS] + m[ROWS:] + sw * bias_ref[1:2, :]
    m = mm(rows[32:64], w1_ref[0:D, :], NT) + mm(rows[64:96], w1_ref[D : 2 * D, :], NT)
    out_ref[0] = (nodes_ref[0].astype(F32) + norm_scale * summed).astype(BF)
    grad_ref[0] = cot_ref[0].astype(F32) + (m[0:ROWS] + m[ROWS:])

    @pl.when(dp > 5)
    def _():
        g1_last[...] = jnp.zeros_like(g1_last)

    @pl.when(dp < 5)
    def _():
        g2_sum[...] = jnp.zeros_like(g2_sum)

    @pl.when(dp >= 5)
    def _():
        acc = gathered(g2_in, 1)
        g2_sum[...] = acc

    for k in range(1, 8):
        arrived(bias_last.at[zat(-k)], b_send.at[k], b_recv.at[k])
    for k in range(8):
        here = jnp.logical_not((z == k) & (c == from_z))

        @pl.when((dp <= 5) & here)
        def _():
            arrived(g1_last.at[k], f_send.at[0], f_recv.at[k])

    g = jnp.concatenate([g1_last[k] for k in range(8)], 1)
    b = jnp.concatenate([bias_last[k] for k in range(8)], 1)
    g = jnp.concatenate(split(jnp.concatenate([g, b, jnp.zeros_like(b)], 0)), 0)
    m = mm(g, perm[...], NT)
    m = m[0:32] + m[32:64]
    g = g2_sum[0:9, :] + m[0:9]
    for k in range(6):
        gsum_ref[pl.ds(k, 9, stride=6), :] = g[:, k * 128 : (k + 1) * 128]
    gsum_ref[54:56, :] = jnp.zeros((2, 128), F32)
    bsum_ref[0:1, :] = m[22:23]
    bsum_ref[2:8, :] = jnp.zeros((6, D), F32)

    for copy, when in pending:
        if when is None:
            copy.wait_send()
        else:
            pl.when(when)(copy.wait_send)


def shards(
    nodes,
    cotangent,
    sources,
    targets,
    edge_weight,
    w_first,
    w_second,
    biases,
    master,
    moment_first,
    moment_second,
    bias_first,
    bias_second,
):
    norm_scale = 1.0 / math.sqrt(sources.shape[1] / nodes.shape[1])
    groups = lax.axis_size("dp")

    def kernel(*refs):
        layer_kernel(norm_scale, *refs)

    vmem = pl.BlockSpec(memory_space=pltpu.VMEM)
    dma = pltpu.SemaphoreType.DMA
    node_out, node_grad, gsum, bsum = pl.pallas_call(
        kernel,
        out_shape=(
            jax.ShapeDtypeStruct((1, ROWS, D), BF),
            jax.ShapeDtypeStruct((1, ROWS, D), F32),
            jax.ShapeDtypeStruct((56, 128), F32),
            jax.ShapeDtypeStruct((8, D), F32),
        ),
        in_specs=[pl.BlockSpec(memory_space=pltpu.HBM)] * 8,
        out_specs=(vmem,) * 4,
        scratch_shapes=[
            pltpu.VMEM((1, ROWS, D), BF),
            pltpu.VMEM((1, ROWS, D), BF),
            pltpu.VMEM((1, EDGE), jnp.int32),
            pltpu.VMEM((1, EDGE), jnp.int32),
            pltpu.VMEM((1, EDGE), F32),
            pltpu.VMEM((2 * D, D), BF),
            pltpu.VMEM((D, D), BF),
            pltpu.VMEM((2, D), F32),
            pltpu.VMEM((2, 2, 2, 128, D), BF),
            pltpu.VMEM((NZ, 16, 128), F32),
            pltpu.VMEM((D, NZ * 128), BF),
            pltpu.VMEM((NZ, 4, ROWS, 128), BF),
            pltpu.VMEM((4, NODES, 128), BF),
            pltpu.VMEM((W, NODES), BF),
            pltpu.VMEM((3 * W, NODES), BF),
            pltpu.VMEM((NZ, NODES, EDGE), BF),
            pltpu.VMEM((NZ, NODES, EDGE), BF),
            pltpu.VMEM((NZ, 8, EDGE), F32),
            pltpu.VMEM((2, 256, 384), F32),
            pltpu.VMEM((2, 256, 384), F32),
            pltpu.VMEM((128, 384), BF),
            pltpu.VMEM((128, 384), BF),
            pltpu.VMEM((128, 384), F32),
            pltpu.VMEM((2, 256, 384), F32),
            pltpu.VMEM((NZ, ROWS, 384), F32),
            pltpu.VMEM((D, NODES), BF),
            pltpu.VMEM((6 * 288, 128), F32),
            pltpu.VMEM((2, 6, 80, 128), BF),
            pltpu.VMEM((16, 80, 128), BF),
            pltpu.VMEM((80, 128), F32),
            pltpu.VMEM((8, ROWS, 128), F32),
            pltpu.VMEM((NZ, ROWS, 128), F32),
            pltpu.VMEM((2, 3, ROWS, D), BF),
            pltpu.VMEM((16, ROWS, D), BF),
            pltpu.VMEM((ROWS, D), F32),
            pltpu.VMEM((8, 128), F32),
            pltpu.VMEM((16, 8, 128), F32),
            pltpu.VMEM((8, 128), F32),
            pltpu.VMEM((NZ, 8, 128), F32),
            dma((2,)),
            dma((2,)),
            dma((2, 4, 2)),
            dma((2, 4, 2)),
            dma((8, 2)),
            dma((8, 2)),
            dma((8,)),
            dma((8,)),
            dma((4, 8)),
            dma((4, 8)),
            dma((3,)),
            dma((3,)),
            dma((8,)),
            dma((8,)),
            dma((3, 8, 2)),
            dma((3, 8, 2)),
            dma((8,)),
            dma((8,)),
            dma((8,)),
            dma((8,)),
            dma((8,)),
        ],
        compiler_params=pltpu.CompilerParams(
            collective_id=0, has_side_effects=True, vmem_limit_bytes=63 * 1024 * 1024
        ),
        name="layer",
    )(nodes, cotangent, sources, targets, edge_weight, w_first, w_second, biases)

    def finish(*refs):
        out, back, grads, bias_grads = refs[0:4]
        refs[10][...] = out[...]
        refs[11][...] = back[...]
        new = adam_update(refs[4][...], refs[5][...], refs[6][...], grads[0:54, :] / groups)
        for ref, value in zip(refs[12:15], new):
            ref[...] = value
        new = adam_update(refs[7][...], refs[8][...], refs[9][...], bias_grads[0:2, :] / groups)
        for ref, value in zip(refs[15:18], new):
            ref[...] = value

    flat = (54, 128)
    done = pl.pallas_call(
        finish,
        out_shape=(
            jax.ShapeDtypeStruct((1, ROWS, D), BF),
            jax.ShapeDtypeStruct((1, ROWS, D), F32),
        )
        + (jax.ShapeDtypeStruct(flat, F32),) * 3
        + (jax.ShapeDtypeStruct((2, D), F32),) * 3,
        name="finish",
    )(
        node_out,
        node_grad,
        gsum,
        bsum,
        master.reshape(flat),
        moment_first.reshape(flat),
        moment_second.reshape(flat),
        biases,
        bias_first,
        bias_second,
    )
    node_out, node_grad = done[0:2]
    new_master, new_first, new_second = [x.reshape(-1) for x in done[2:5]]
    new_biases, new_bias_first, new_bias_second = done[5:8]
    return (
        node_out,
        node_grad,
        new_master,
        new_first,
        new_second,
        new_biases,
        new_bias_first,
        new_bias_second,
    )


def solution(mesh):
    placed = (
        P("dp", "graph", None),
        P("dp", "graph", None),
        P("dp", "graph"),
        P("dp", "graph"),
        P("dp", "graph"),
        P(),
        P(),
        P(),
        P(("dp", "graph")),
        P(("dp", "graph")),
        P(("dp", "graph")),
        P(),
        P(),
    )
    return jax.shard_map(
        shards,
        mesh=mesh,
        in_specs=placed,
        out_specs=(
            P("dp", "graph", None),
            P("dp", "graph", None),
            P(("dp", "graph")),
            P(("dp", "graph")),
            P(("dp", "graph")),
            P(),
            P(),
            P(),
        ),
        check_vma=False,
    )
```

```python
import math

import jax
import jax.numpy as jnp
from jax import lax
from jax.experimental import pallas as pl
from jax.experimental.pallas import tpu as pltpu
from jax.sharding import PartitionSpec as P

STEP = 10


beta_one = 0.9
beta_two = 0.999
epsilon = 1e-08
learn_rate = 0.001

D = 768
ROWS = 16
EDGE = 1024
NZ = 8
ORDER = (4, 5, 3, 6, 2, 7, 1)
W = 112
NODES = 512
BF = jnp.bfloat16
F32 = jnp.float32
NN = (((1,), (0,)), ((), ()))
NT = (((1,), (1,)), ((), ()))
TN = (((0,), (0,)), ((), ()))


def mm(a, b, dims=NN):
    return lax.dot_general(a, b, dims, preferred_element_type=F32)


def split(x):
    hi = x.astype(BF)
    return hi, (x - hi.astype(F32)).astype(BF)


def adam_update(param, first, second, grads):
    new_first = beta_one * first + (1.0 - beta_one) * grads
    new_second = beta_two * second + (1.0 - beta_two) * grads * grads
    ratio = (
        new_first
        / (1.0 - beta_one**STEP)
        / (jnp.sqrt(new_second / (1.0 - beta_two**STEP)) + epsilon)
    )
    return (param - learn_rate * ratio, new_first, new_second)


def column_of(z, i):
    owner = ((i % 36) // 18) * 16 + z * 2 + ((i % 18) // 9)
    h = (5 + i // 36) * 288 + owner * 9 + i % 9 - 2 * D
    return jnp.where((i < 108) & (h >= 0), h, -1)


def layer_kernel(
    norm_scale,
    nodes_hbm,
    cot_hbm,
    src_hbm,
    tgt_hbm,
    weight_hbm,
    w1_hbm,
    w2_hbm,
    bias_hbm,
    out_ref,
    grad_ref,
    gsum_ref,
    bsum_ref,
    nodes_ref,
    cot_ref,
    src_ref,
    tgt_ref,
    weight_ref,
    w1_ref,
    w2_ref,
    bias_ref,
    feats,
    edges,
    perm,
    prod_out,
    prod,
    psrc,
    ptgt,
    onehot_s,
    onehot_t,
    row,
    part,
    part_in,
    half_out,
    half_in,
    nodes_sum,
    total,
    own,
    flip,
    g1,
    g1_half,
    g1_in,
    g1_sum,
    g1_out,
    g1_last,
    g2,
    g2_in,
    g2_sum,
    bias_out,
    bias_in,
    bias_mine,
    bias_last,
    y_send,
    y_recv,
    z_send,
    z_recv,
    c_send,
    c_recv,
    e_send,
    e_recv,
    p_send,
    p_recv,
    r_send,
    r_recv,
    a_send,
    a_recv,
    d_send,
    d_recv,
    f_send,
    f_recv,
    b_send,
    b_recv,
    l_sem,
):
    dp = lax.axis_index("dp")
    graph = lax.axis_index("graph")
    y = graph // 16
    z = (graph // 2) % 8
    c = graph % 2
    quarter = y * 2 + c

    def peer(py, pz, pc):
        return {"dp": dp, "graph": py * 16 + pz * 2 + pc}

    def zat(k):
        return (z + k + 8) % 8

    y_peer = peer(1 - y, z, c)
    c_peer = peer(y, z, 1 - c)
    right = peer(y, zat(1), c)
    left = peer(y, zat(-1), c)

    loads = [
        pltpu.make_async_copy(src, dst, l_sem.at[i])
        for i, (src, dst) in enumerate(
            [
                (nodes_hbm, nodes_ref),
                (cot_hbm, cot_ref),
                (src_hbm, src_ref),
                (tgt_hbm, tgt_ref),
                (weight_hbm, weight_ref),
                (bias_hbm, bias_ref),
                (w1_hbm, w1_ref),
                (w2_hbm, w2_ref),
            ]
        )
    ]
    for load in loads:
        load.start()

    barrier = pltpu.get_barrier_semaphore()
    greet = [y_peer, c_peer]
    for k in range(1, 8):
        greet += [peer(y, zat(k), c), peer(y, zat(k), 1 - c)]
        greet += [{"dp": (dp + k) % 8, "graph": h * 16 + z * 2 + c} for h in range(2)]
    for who in greet:
        pl.semaphore_signal(barrier, inc=1, device_id=who, device_id_type=pl.DeviceIdType.MESH)

    def remote(src, dst, send, recv, who):
        return pltpu.make_async_remote_copy(
            src_ref=src,
            dst_ref=dst,
            send_sem=send,
            recv_sem=recv,
            device_id=who,
            device_id_type=pl.DeviceIdType.MESH,
        )

    pending = []

    def send(src, dst, ssem, rsem, who, when=None):
        copy = remote(src, dst, ssem, rsem, who)
        if when is None:
            copy.start()
        else:
            pl.when(when)(copy.start)
        pending.append((copy, when))

    def arrived(dst, ssem, rsem):
        remote(dst, dst, ssem, rsem, right).wait_recv()

    at_h = lax.broadcasted_iota(jnp.int32, (D, 128), 0)
    for k in range(8):
        place_of = column_of(k, lax.broadcasted_iota(jnp.int32, (1, 128), 1))
        perm[:, k * 128 : (k + 1) * 128] = jnp.where(at_h == place_of, 1.0, 0.0).astype(BF)

    for load in loads[0:5]:
        load.wait()
    zrow = pl.multiple_of(z * ROWS, ROWS)
    feats[0, c, y, pl.ds(zrow, ROWS), :] = nodes_ref[0]
    feats[1, c, y, pl.ds(zrow, ROWS), :] = cot_ref[0]

    def place(n):
        ny, nz, nc, nr = n // 256, (n // 32) % 8, (n // 16) % 2, n % 16
        return nc * 256 + ny * 128 + nz * 16 + nr

    for j in range(8):
        lanes = slice(j * 128, (j + 1) * 128)
        ends = place(src_ref[0:1, lanes]) + NODES * place(tgt_ref[0:1, lanes])
        edges[z, j : j + 1, :] = ends.astype(F32)
        edges[z, 8 + j : 9 + j, :] = weight_ref[0:1, lanes]

    for load in loads[5:8]:
        load.wait()
    from_s = mm(nodes_ref[0], w1_ref[0:D, :]).astype(BF)
    from_t = split(mm(nodes_ref[0], w1_ref[D : 2 * D, :]))
    from_c = (norm_scale * mm(cot_ref[0], w2_ref[...], NT)).astype(BF)
    stack = jnp.concatenate([from_s, from_t[0], from_t[1], from_c], 0)
    spread = mm(stack, perm[...])
    for k in range(8):
        for kind in range(4):
            rows = slice(kind * ROWS, (kind + 1) * ROWS)
            prod_out[k, kind] = spread[rows, k * 128 : (k + 1) * 128].astype(BF)

    pl.semaphore_wait(barrier, len(greet))

    def zbase(pc, py, pz):
        return pl.multiple_of(pc * 256 + py * 128 + pz * ROWS, ROWS)

    def products(pc, py, pz):
        return prod.at[:, pl.ds(zbase(pc, py, pz), ROWS), :]

    for kind in range(2):
        mine = feats.at[kind, c, y, pl.ds(zrow, ROWS), :]
        send(mine, mine, y_send.at[kind], y_recv.at[kind], y_peer)
    for k in ORDER:
        to = peer(y, zat(k), c)
        send(prod_out.at[zat(k)], products(c, y, z), p_send.at[0, k], p_recv.at[0, k], to)
    for k in ORDER:
        send(edges.at[z], edges.at[z], e_send.at[k], e_recv.at[k], peer(y, zat(k), c))
    prod[:, pl.ds(zbase(c, y, z), ROWS), :] = prod_out[z]

    def slot(kind, at):
        return feats.at[kind, c, :, pl.ds(pl.multiple_of(at * ROWS, ROWS), ROWS), :]

    def other_slot(kind, at):
        return feats.at[kind, 1 - c, :, pl.ds(pl.multiple_of(at * ROWS, ROWS), ROWS), :]

    def to_right(kind, k):
        ref = slot(kind, zat(-k))
        send(ref, ref, z_send.at[0, k, kind], z_recv.at[0, k, kind], right)

    def to_left(kind, k):
        ref = slot(kind, zat(k))
        send(ref, ref, z_send.at[1, k, kind], z_recv.at[1, k, kind], left)

    def to_core(kind, k):
        ref = slot(kind, zat(k))
        send(ref, ref, c_send.at[k % 8, kind], c_recv.at[k % 8, kind], c_peer)

    def ring(k):
        for kind in range(2):
            arrived(slot(kind, zat(-k)), z_send.at[0, k - 1, kind], z_recv.at[0, k - 1, kind])
            if k < 4:
                to_right(kind, k)
            to_core(kind, -k)
            if k < 4:
                arrived(slot(kind, zat(k)), z_send.at[1, k - 1, kind], z_recv.at[1, k - 1, kind])
                if k < 3:
                    to_left(kind, k)
                to_core(kind, k)

    pick = lax.broadcasted_iota(jnp.int32, (W, D), 1) == column_of(
        z, lax.broadcasted_iota(jnp.int32, (W, 1), 0)
    )
    b0 = jnp.sum(jnp.where(pick, bias_ref[0:1, :], 0.0), axis=1, keepdims=True)

    def build(i):
        ids = lax.broadcasted_iota(jnp.int32, (NODES, 128), 0)
        for j in range(8):
            lanes = slice(j * 128, (j + 1) * 128)
            ends = edges[i, j : j + 1, :].astype(jnp.int32)
            onehot_s[i, :, lanes] = jnp.where(ids == (ends & (NODES - 1)), 1.0, 0.0).astype(BF)
            onehot_t[i, :, lanes] = jnp.where(ids == (ends >> 9), 1.0, 0.0).astype(BF)
            row[i, 0:1, lanes] = edges[i, 8 + j : 9 + j, :]

    def onward(k):
        ref = products(c, y, zat(-k))
        if k:
            arrived(ref, p_send.at[0, k], p_recv.at[0, k])
        send(ref, ref, p_send.at[1, k], p_recv.at[1, k], y_peer)
        send(ref, ref, p_send.at[2, k], p_recv.at[2, k], c_peer)

    near = ORDER[::-1]
    onward(0)
    build(z)
    for k in near:
        onward(k)
        if k == near[1]:
            for kind in range(2):
                theirs = feats.at[kind, c, 1 - y, pl.ds(zrow, ROWS), :]
                arrived(theirs, y_send.at[kind], y_recv.at[kind])
                to_right(kind, 0)
                to_left(kind, 0)
                to_core(kind, 0)
    for k in near:
        arrived(edges.at[zat(-k)], e_send.at[k], e_recv.at[k])
        build(zat(-k))
    for k in (0,) + near:
        ref = products(c, 1 - y, zat(-k))
        arrived(ref, p_send.at[1, k], p_recv.at[1, k])
        send(ref, ref, p_send.at[3, k], p_recv.at[3, k], c_peer)
    for k in range(8):
        arrived(products(1 - c, y, zat(-k)), p_send.at[2, k], p_recv.at[2, k])
        arrived(products(1 - c, 1 - y, zat(-k)), p_send.at[3, k], p_recv.at[3, k])

    ring(1)
    psrc[...] = prod[0].astype(F32).T[0:W].astype(BF)
    for kind in range(3):
        ptgt[kind * W : (kind + 1) * W] = prod[kind + 1].astype(F32).T[0:W].astype(BF)

    def edge_block(i):
        w = row[i, 0:1, :]
        u = mm(psrc[...], onehot_s[i])
        v = mm(ptgt[...], onehot_t[i])
        pre = (u + v[0:W]) + v[W : 2 * W] + b0
        sg = 0.5 * jnp.tanh(0.5 * pre) + 0.5
        act = pre * sg
        dpre = ((v[2 * W : 3 * W] * w) * (sg * (1.0 + pre - act))).astype(BF)
        w_hi, w_lo = split(w)
        rank = lax.broadcasted_iota(jnp.int32, (128 - W, EDGE), 0)
        tail = jnp.where(rank == 0, w_hi.astype(F32), jnp.where(rank == 1, w_lo.astype(F32), 0.0))
        zeros = jnp.zeros((128 - W, EDGE), BF)
        to_t = jnp.concatenate([(act * w).astype(BF), tail.astype(BF), dpre, zeros], 0)
        to_s = jnp.concatenate([dpre, zeros], 0)
        return mm(onehot_t[i], to_t, NT), mm(onehot_s[i], to_s, NT)

    def edge_group(blocks, first):
        sums_of = [edge_block(i) for i in blocks]
        at, s = sum(t for t, _ in sums_of), sum(s for _, s in sums_of)
        for h in range(2):
            rows = slice(h * 256, (h + 1) * 256)
            for to, x in ((0, at[rows, 0:128]), (256, at[rows, 128:256]), (128, s[rows, :])):
                lanes = slice(to, to + 128)
                part[h, :, lanes] = x if first else part[h, :, lanes] + x

    edge_group((0, 1, 2), True)
    ring(2)
    edge_group((3, 4, 5), False)
    ring(3)
    edge_group((6, 7), False)

    send(part, part_in, r_send.at[0], r_recv.at[0], c_peer)
    ring(4)

    for kind in range(2):
        for k in range(8):
            arrived(other_slot(kind, zat(k)), c_send.at[k, kind], c_recv.at[k, kind])
    flip[...] = feats[0].reshape(NODES, D).astype(F32).T.astype(BF)
    lane = lax.broadcasted_iota(jnp.int32, (96, 128), 1)
    mine = lax.broadcasted_iota(jnp.int32, (96, 128), 0)
    of_y = (mine // 48) * 18 + c * 9
    wanted = jnp.where(mine % 16 < 9, (mine % 48 // 16) * 36 + of_y + mine % 16, -1)
    chosen = jnp.where(lane == wanted, 1.0, 0.0).astype(BF)

    arrived(part_in, r_send.at[0], r_recv.at[0])
    total[...] = part[...] + part_in[...]
    half_out[...] = total[c, pl.ds(pl.multiple_of((1 - y) * 128, 128), 128), :].astype(BF)
    send(half_out, half_in, r_send.at[1], r_recv.at[1], y_peer)

    def sums(kind):
        return total[:, :, kind * 128 : (kind + 1) * 128].reshape(NODES, 128)

    sum_a, sum_s, sum_t = sums(0), sums(1), sums(2)
    for kind, x in enumerate((sum_s, sum_t)):
        m = mm(flip[...], jnp.concatenate(split(x), 1))
        g1[kind * D : (kind + 1) * D, :] = m[:, 0:128] + m[:, 128:256]
    g1[2 * D :, :] = jnp.zeros((6 * 288 - 2 * D, 128), F32)

    for h in range(2):
        for d in range(6):
            at = pl.ds(pl.multiple_of(d * 288 + h * 144 + c * 72, 8), 72)
            rows = jnp.concatenate([g1[at, :], jnp.zeros((8, 128), F32)], 0)
            g1_half[h, d] = rows.astype(BF)

    others = []
    for k in range(8):
        for h in range(2):
            if k or h:
                to, ty = (dp + k) % 8, (y + h) % 2
                others.append((k, h, to, ty, {"dp": to, "graph": ty * 16 + z * 2 + c}))

    me = dp * 2 + y
    for k, h, to, ty, who in others:
        src = g1_half.at[ty, jnp.minimum(to, 5)]
        send(src, g1_in.at[me], d_send.at[0, k, h], d_recv.at[0, k, h], who, to <= 5)

    arrived(half_in, r_send.at[1], r_recv.at[1])
    nodes_sum[...] = total[c, pl.ds(pl.multiple_of(y * 128, 128), 128), :] + half_in[...].astype(F32)
    own[z] = nodes_sum[pl.ds(zrow, ROWS), :]
    for k in range(1, 8):
        rows = pl.ds(pl.multiple_of(zat(k) * ROWS, ROWS), ROWS)
        send(nodes_sum.at[rows, :], own.at[z], a_send.at[k], a_recv.at[k], peer(y, zat(k), c))

    hi, lo = split(sum_a)
    all_cot = feats[1].reshape(NODES, D)
    rows_a = jnp.concatenate([mm(chosen, hi, NT), mm(chosen, lo, NT)], 0).astype(BF)
    m = norm_scale * mm(rows_a, all_cot)
    g2[...] = (m[0:96] + m[96:192]).reshape(2, 3, ROWS, D).astype(BF)
    for k, h, to, ty, who in others:
        src = g2.at[ty, jnp.maximum(to - 5, 0)]
        send(src, g2_in.at[me], d_send.at[1, k, h], d_recv.at[1, k, h], who, to >= 5)

    weights = hi.astype(F32).T[W : W + 16], lo.astype(F32).T[W : W + 16]
    m = norm_scale * mm(jnp.concatenate(weights, 0).astype(BF), all_cot)
    second = (m[0:1] + m[1:2]) + (m[16:17] + m[17:18])
    for k in range(6):
        bias_out[k : k + 1, :] = second[:, k * 128 : (k + 1) * 128]
    bias_out[6:7, :] = jnp.sum(sum_t, axis=0, keepdims=True)
    bias_out[7:8, :] = jnp.zeros((1, 128), F32)
    bias_in[me] = bias_out[...]
    for k, h, to, ty, who in others:
        send(bias_out, bias_in.at[me], d_send.at[2, k, h], d_recv.at[2, k, h], who)

    @pl.when(dp <= 5)
    def _():
        g1_in[me] = g1_half[y, jnp.minimum(dp, 5)]

    @pl.when(dp >= 5)
    def _():
        g2_in[me] = g2[y, jnp.maximum(dp - 5, 0)]

    def gathered(ref, stage):
        for k, h, to, ty, who in others:
            at = ((dp - k + 8) % 8) * 2 + (y + h) % 2
            arrived(ref.at[at], d_send.at[stage, k, h], d_recv.at[stage, k, h])
        acc = ref[0].astype(F32)
        for k in range(1, 16):
            acc += ref[k].astype(F32)
        return acc

    from_z = z // 4

    @pl.when(dp <= 5)
    def _():
        acc = gathered(g1_in, 0)
        g1_sum[...] = acc
        for j in range(8):
            g1_out[j, 0:9, :] = g1_sum[9 * j : 9 * j + 9, :]
            g1_out[j, 9:16, :] = jnp.zeros((7, 128), F32)

    for j in range(8):
        elsewhere = jnp.logical_not((z == 4 * c + j // 2) & (c == j % 2))
        send(
            g1_out.at[j],
            g1_last.at[z],
            f_send.at[j],
            f_recv.at[z],
            {"dp": dp, "graph": 8 * quarter + j},
            (dp <= 5) & elsewhere,
        )

    @pl.when((dp <= 5) & (c == from_z))
    def _():
        g1_last[z] = g1_out[(z % 4) * 2 + c]

    acc = gathered(bias_in, 2)
    bias_mine[...] = acc
    bias_last[z] = acc
    for k in range(1, 8):
        send(bias_mine, bias_last.at[z], b_send.at[k], b_recv.at[k], peer(y, zat(k), c))
    for k in range(6):
        bsum_ref[1:2, k * 128 : (k + 1) * 128] = acc[k : k + 1, :]

    for k in range(1, 8):
        arrived(own.at[zat(-k)], a_send.at[k], a_recv.at[k])
    pieces = []
    for kind in range(3):
        x = jnp.concatenate([own[k, :, kind * 128 : (kind + 1) * 128] for k in range(8)], 1)
        pieces += split(x)
    rows = mm(jnp.concatenate(pieces, 0), perm[...], NT).astype(BF)
    m = mm(rows[0:32], w2_ref[...])
    sw = own[0, :, W : W + 1] + own[0, :, W + 1 : W + 2]
    summed = m[0:ROWS] + m[ROWS:] + sw * bias_ref[1:2, :]
    m = mm(rows[32:64], w1_ref[0:D, :], NT) + mm(rows[64:96], w1_ref[D : 2 * D, :], NT)
    out_ref[0] = (nodes_ref[0].astype(F32) + norm_scale * summed).astype(BF)
    grad_ref[0] = cot_ref[0].astype(F32) + (m[0:ROWS] + m[ROWS:])

    @pl.when(dp > 5)
    def _():
        g1_last[...] = jnp.zeros_like(g1_last)

    @pl.when(dp < 5)
    def _():
        g2_sum[...] = jnp.zeros_like(g2_sum)

    @pl.when(dp >= 5)
    def _():
        acc = gathered(g2_in, 1)
        g2_sum[...] = acc

    for k in range(1, 8):
        arrived(bias_last.at[zat(-k)], b_send.at[k], b_recv.at[k])
    for k in range(8):
        here = jnp.logical_not((z == k) & (c == from_z))

        @pl.when((dp <= 5) & here)
        def _():
            arrived(g1_last.at[k], f_send.at[0], f_recv.at[k])

    g = jnp.concatenate([g1_last[k] for k in range(8)], 1)
    b = jnp.concatenate([bias_last[k] for k in range(8)], 1)
    g = jnp.concatenate(split(jnp.concatenate([g, b, jnp.zeros_like(b)], 0)), 0)
    m = mm(g, perm[...], NT)
    m = m[0:32] + m[32:64]
    g = g2_sum[0:9, :] + m[0:9]
    for k in range(6):
        gsum_ref[pl.ds(k, 9, stride=6), :] = g[:, k * 128 : (k + 1) * 128]
    gsum_ref[54:56, :] = jnp.zeros((2, 128), F32)
    bsum_ref[0:1, :] = m[22:23]
    bsum_ref[2:8, :] = jnp.zeros((6, D), F32)

    for copy, when in pending:
        if when is None:
            copy.wait_send()
        else:
            pl.when(when)(copy.wait_send)


def shards(
    nodes,
    cotangent,
    sources,
    targets,
    edge_weight,
    w_first,
    w_second,
    biases,
    master,
    moment_first,
    moment_second,
    bias_first,
    bias_second,
):
    norm_scale = 1.0 / math.sqrt(sources.shape[1] / nodes.shape[1])
    groups = lax.axis_size("dp")

    def kernel(*refs):
        layer_kernel(norm_scale, *refs)

    vmem = pl.BlockSpec(memory_space=pltpu.VMEM)
    dma = pltpu.SemaphoreType.DMA
    node_out, node_grad, gsum, bsum = pl.pallas_call(
        kernel,
        out_shape=(
            jax.ShapeDtypeStruct((1, ROWS, D), BF),
            jax.ShapeDtypeStruct((1, ROWS, D), F32),
            jax.ShapeDtypeStruct((56, 128), F32),
            jax.ShapeDtypeStruct((8, D), F32),
        ),
        in_specs=[pl.BlockSpec(memory_space=pltpu.HBM)] * 8,
        out_specs=(vmem,) * 4,
        scratch_shapes=[
            pltpu.VMEM((1, ROWS, D), BF),
            pltpu.VMEM((1, ROWS, D), BF),
            pltpu.VMEM((1, EDGE), jnp.int32),
            pltpu.VMEM((1, EDGE), jnp.int32),
            pltpu.VMEM((1, EDGE), F32),
            pltpu.VMEM((2 * D, D), BF),
            pltpu.VMEM((D, D), BF),
            pltpu.VMEM((2, D), F32),
            pltpu.VMEM((2, 2, 2, 128, D), BF),
            pltpu.VMEM((NZ, 16, 128), F32),
            pltpu.VMEM((D, NZ * 128), BF),
            pltpu.VMEM((NZ, 4, ROWS, 128), BF),
            pltpu.VMEM((4, NODES, 128), BF),
            pltpu.VMEM((W, NODES), BF),
            pltpu.VMEM((3 * W, NODES), BF),
            pltpu.VMEM((NZ, NODES, EDGE), BF),
            pltpu.VMEM((NZ, NODES, EDGE), BF),
            pltpu.VMEM((NZ, 8, EDGE), F32),
            pltpu.VMEM((2, 256, 384), F32),
            pltpu.VMEM((2, 256, 384), F32),
            pltpu.VMEM((128, 384), BF),
            pltpu.VMEM((128, 384), BF),
            pltpu.VMEM((128, 384), F32),
            pltpu.VMEM((2, 256, 384), F32),
            pltpu.VMEM((NZ, ROWS, 384), F32),
            pltpu.VMEM((D, NODES), BF),
            pltpu.VMEM((6 * 288, 128), F32),
            pltpu.VMEM((2, 6, 80, 128), BF),
            pltpu.VMEM((16, 80, 128), BF),
            pltpu.VMEM((80, 128), F32),
            pltpu.VMEM((8, ROWS, 128), F32),
            pltpu.VMEM((NZ, ROWS, 128), F32),
            pltpu.VMEM((2, 3, ROWS, D), BF),
            pltpu.VMEM((16, ROWS, D), BF),
            pltpu.VMEM((ROWS, D), F32),
            pltpu.VMEM((8, 128), F32),
            pltpu.VMEM((16, 8, 128), F32),
            pltpu.VMEM((8, 128), F32),
            pltpu.VMEM((NZ, 8, 128), F32),
            dma((2,)),
            dma((2,)),
            dma((2, 4, 2)),
            dma((2, 4, 2)),
            dma((8, 2)),
            dma((8, 2)),
            dma((8,)),
            dma((8,)),
            dma((4, 8)),
            dma((4, 8)),
            dma((3,)),
            dma((3,)),
            dma((8,)),
            dma((8,)),
            dma((3, 8, 2)),
            dma((3, 8, 2)),
            dma((8,)),
            dma((8,)),
            dma((8,)),
            dma((8,)),
            dma((8,)),
        ],
        compiler_params=pltpu.CompilerParams(
            collective_id=0, has_side_effects=True, vmem_limit_bytes=63 * 1024 * 1024
        ),
        name="layer",
    )(nodes, cotangent, sources, targets, edge_weight, w_first, w_second, biases)

    def finish(*refs):
        out, back, grads, bias_grads = refs[0:4]
        refs[10][...] = out[...]
        refs[11][...] = back[...]
        new = adam_update(refs[4][...], refs[5][...], refs[6][...], grads[0:54, :] / groups)
        for ref, value in zip(refs[12:15], new):
            ref[...] = value
        new = adam_update(refs[7][...], refs[8][...], refs[9][...], bias_grads[0:2, :] / groups)
        for ref, value in zip(refs[15:18], new):
            ref[...] = value

    flat = (54, 128)
    done = pl.pallas_call(
        finish,
        out_shape=(
            jax.ShapeDtypeStruct((1, ROWS, D), BF),
            jax.ShapeDtypeStruct((1, ROWS, D), F32),
        )
        + (jax.ShapeDtypeStruct(flat, F32),) * 3
        + (jax.ShapeDtypeStruct((2, D), F32),) * 3,
        name="finish",
    )(
        node_out,
        node_grad,
        gsum,
        bsum,
        master.reshape(flat),
        moment_first.reshape(flat),
        moment_second.reshape(flat),
        biases,
        bias_first,
        bias_second,
    )
    node_out, node_grad = done[0:2]
    new_master, new_first, new_second = [x.reshape(-1) for x in done[2:5]]
    new_biases, new_bias_first, new_bias_second = done[5:8]
    return (
        node_out,
        node_grad,
        new_master,
        new_first,
        new_second,
        new_biases,
        new_bias_first,
        new_bias_second,
    )


def solution(mesh):
    placed = (
        P("dp", "graph", None),
        P("dp", "graph", None),
        P("dp", "graph"),
        P("dp", "graph"),
        P("dp", "graph"),
        P(),
        P(),
        P(),
        P(("dp", "graph")),
        P(("dp", "graph")),
        P(("dp", "graph")),
        P(),
        P(),
    )
    return jax.shard_map(
        shards,
        mesh=mesh,
        in_specs=placed,
        out_specs=(
            P("dp", "graph", None),
            P("dp", "graph", None),
            P(("dp", "graph")),
            P(("dp", "graph")),
            P(("dp", "graph")),
            P(),
            P(),
            P(),
        ),
        check_vma=False,
    )
```
